32 devices in a mesh: groups: 2 (over x), gx: 16 (over z, y, core).
Axes of the slice: x: 2, y: 2, z: 4, core: 2. Of those that a mesh axis runs over, the one named last changes fastest.
Arguments:
- samples: bfloat16 [2, 2048, 67328], P(None, ('groups', 'gx')), parts along dimension 1, may hold values from -6 to 6
- flags: int32 [1024], P('gx'), may hold values 0 or 1
- kept_channels: int32 [192], replicated, may hold values from 0 to 255, as said below
- beam_order: int32 [256], replicated, may hold values from 0 to 255, each once
- dm_bins: int32 [512], P('groups'), parts along dimension 0, may hold values from 0 to 4095
- delays: float32 [512, 1024], P('groups'), parts along dimension 0, may hold values from -64 to 64
Outputs:
- visibilities: bfloat16 [384, 1024, 1024], P(('groups', 'gx')), parts along dimension 0
- beam_series: float32 [2, 512, 256, 256], P(None, ('groups', 'gx')), parts along dimension 1
The draws below stay inside these ranges and needn't reach their ends.
There are 2 independent parts, one for each index of `groups`. The reference program is written for one: setup_inputs(seed, part) draws one part's arguments, and reference() takes and returns one part's arrays. A program takes and returns all parts, laid end to end along the dimension named above; an argument that names none is the same for every part. Nothing has to cross between parts.
Inputs may be any that keep to these rules, and one draw needn't show every extreme that they name: `kept_channels`: 192 different bins in increasing order, always including 0 and 255.
All inputs are finite; a program needn't handle non-finite values. No bound on the sum of `flags` on one device may be relied on, other than what follows from the above.
Results may differ from the reference program's by a relative error of at most 0.0075.
Values may be sent and summed in bfloat16 or wider, within the bound.
No kernel may reach another device: no remote copies, remote signals or barrier semaphores. Data moves between devices by JAX's collectives and lax.ppermute only.
A program may use at most 320 MiB of HBM per device.

```python
import math
import jax
import jax.numpy as jnp
from jax import lax

INPUTS = 1024
POINTS = 256
CHANNELS = 192
BEAMS = 256
TAPS = 8
SPECTRA = 256
NSAMP = 67328


def draw_kept_channels(key, part):
    key = jax.random.fold_in(key, 11)
    middle_set = jax.random.permutation(key, POINTS - 2)[:CHANNELS - 2] + 1
    chosen = jnp.concatenate([jnp.zeros((1,), jnp.int32), middle_set.astype(jnp.int32), jnp.full((1,), POINTS - 1, jnp.int32)])
    return jnp.sort(chosen).astype(jnp.int32)


def with_ends(values, key, least, high):
    dims = values.shape
    spot = [jax.random.randint(jax.random.fold_in(key, axis), (), 0, dims[axis]) for axis in range(len(dims))]
    values = values.at[tuple(spot)].set(least)
    longest = dims.index(max(dims))
    spot[longest] = (spot[longest] + 1) % dims[longest]
    return values.at[tuple(spot)].set(high)


def steps_of(key, dims, split, least, top_value):
    def one(dim, parts):
        heights = jax.random.uniform(jax.random.fold_in(jax.random.fold_in(key, 6), dim), (parts,), jnp.float32, least / len(split), top_value / len(split))
        return jnp.repeat(jnp.exp(heights), dims[dim] // parts).reshape((-1,) + (1,) * (len(dims) - dim - 1))

    factor_of = one(*split[0])
    for cut in split[1:]:
        factor_of = factor_of * one(*cut)
    return factor_of


def scatter_about(own_key, shape, scale, most, split=(), held_as=jnp.bfloat16):
    array = scale * jax.random.normal(own_key, shape, jnp.float32)
    if split:
        array = array * steps_of(own_key, shape, split, -0.22, 0.18)
    return jnp.clip(array, -most, most).astype(held_as)


def setup_inputs(seed: int = 0, part: int = 0) -> dict:
    splits = jax.random.split(jax.random.key(seed), 7)
    part_keys = jax.random.split(jax.random.fold_in(splits[6], part), 7)
    return {
        "samples": scatter_about(part_keys[0], (2, INPUTS, NSAMP), 1.0, 6.0, ((1, 16),)),
        "flags": with_ends((jax.random.randint(splits[1], (INPUTS,), 0, 8) < 7).astype(jnp.int32), jax.random.fold_in(splits[1], 1), 0, 1),
        "kept_channels": draw_kept_channels(jax.random.fold_in(splits[6], 71), part),
        "beam_order": jax.random.permutation(splits[3], BEAMS).astype(jnp.int32),
        "dm_bins": with_ends(jax.random.randint(part_keys[4], (BEAMS,), 0, 4096), jax.random.fold_in(part_keys[4], 1), 0, 4095).astype(jnp.int32),
        "delays": jnp.clip(jax.random.uniform(part_keys[5], (BEAMS, INPUTS), jnp.float32, -64.0, 64.0), -64.0, 64.0),
    }


def prototype_taper(tap_count, point_count):
    spots = jnp.arange(tap_count * point_count, dtype=jnp.float32)
    length = float(tap_count * point_count)
    shaped = jnp.sinc((spots - length / 2.0 + 0.5) / point_count) * (0.5 - 0.5 * jnp.cos(2.0 * math.pi * (spots + 0.5) / length))
    return shaped.reshape(tap_count, point_count)

def filterbank(samples, taper, start, count):
    point_count = taper.shape[1]
    blocks = samples.reshape(samples.shape[0], samples.shape[1], -1, point_count)
    summed = jnp.zeros((blocks.shape[0], blocks.shape[1], count, point_count), jnp.float32)
    for tap_index in range(taper.shape[0]):
        window = blocks[:, :, start + tap_index:start + tap_index + count, :]
        summed = summed + window.astype(jnp.float32) * taper[tap_index]
    return summed.astype(jnp.bfloat16)

def dft_tables(kept, point_count):
    spots = jnp.arange(point_count, dtype=jnp.int32)
    turns = kept.astype(jnp.int32)[:, None] * spots[None, :] % point_count
    angle = turns.astype(jnp.float32) * (2.0 * math.pi / point_count)
    scale = 1.0 / math.sqrt(point_count)
    cosine = jnp.cos(angle) * scale
    sine = jnp.sin(angle) * scale
    analysis = jnp.stack([jnp.stack([cosine, sine], 1), jnp.stack([-sine, cosine], 1)], 1).astype(jnp.bfloat16)
    synthesis = jnp.stack([jnp.stack([cosine, -sine], 0), jnp.stack([sine, cosine], 0)], 0).astype(jnp.bfloat16)
    return (analysis, synthesis)

def beam_weights(kept_part, tau_rows, point_count, input_count):
    angle = kept_part.astype(jnp.float32)[:, None, None] * tau_rows[None, :, :] * (2.0 * math.pi / point_count)
    scale = 1.0 / math.sqrt(input_count)
    return ((jnp.cos(angle) * scale).astype(jnp.bfloat16), (-jnp.sin(angle) * scale).astype(jnp.bfloat16))

def rotation(dm_rows, kept):
    kept_int = kept.astype(jnp.int32)
    squares = kept_int * kept_int % 4096
    turns = squares[:, None] * dm_rows.astype(jnp.int32)[None, :] % 4096
    angle = turns.astype(jnp.float32) * (2.0 * math.pi / 4096.0)
    return (jnp.cos(angle), jnp.sin(angle))

def rotate(beam_sums, cosine, sine):
    real_part = beam_sums[:, 0].astype(jnp.float32)
    imag_part = beam_sums[:, 1].astype(jnp.float32)
    cos_wide = cosine[:, :, None]
    sin_wide = sine[:, :, None]
    first = real_part * cos_wide + imag_part * sin_wide
    second = imag_part * cos_wide - real_part * sin_wide
    return jnp.stack([first, second], 1).astype(jnp.bfloat16)

def reference(samples, flags, kept_channels, beam_order, dm_bins, delays):
    taper = prototype_taper(TAPS, POINTS)
    frames = filterbank(samples, taper, 0, SPECTRA)
    analysis, synthesis = dft_tables(kept_channels, POINTS)
    spectra = jnp.einsum('coxn,xisn->cois', analysis.astype(jnp.float32), frames.astype(jnp.float32))
    spectra = (spectra * flags.astype(jnp.float32)[None, None, :, None]).astype(jnp.bfloat16)
    upper_mask = jnp.arange(INPUTS)[:, None] <= jnp.arange(INPUTS)[None, :]

    def one_gram(channel_spectra):
        values = channel_spectra.astype(jnp.float32)
        joined = jnp.concatenate([values[0], values[1]], axis=1)
        real_sum = jnp.dot(joined, joined.T, preferred_element_type=jnp.float32)
        mixed = jnp.dot(values[1], values[0].T, preferred_element_type=jnp.float32)
        packed = jnp.where(upper_mask, real_sum, mixed - mixed.T)
        return (packed / SPECTRA).astype(jnp.bfloat16)
    visibilities = lax.map(one_gram, spectra)
    tau_rows = jnp.take(delays, beam_order, axis=0)

    def one_beam(item):
        kept_one, channel_spectra = item
        weight_real, weight_imag = beam_weights(kept_one[None], tau_rows, POINTS, INPUTS)
        values = channel_spectra.astype(jnp.float32)
        first = jnp.einsum('bi,xis->xbs', weight_real[0].astype(jnp.float32), values)
        second = jnp.einsum('bi,xis->xbs', weight_imag[0].astype(jnp.float32), values)
        return jnp.stack([first[0] - second[1], first[1] + second[0]], 0).astype(jnp.bfloat16)
    beam_sums = lax.map(one_beam, (kept_channels, spectra))
    cosine, sine = rotation(jnp.take(dm_bins, beam_order), kept_channels)
    rotated = rotate(beam_sums, cosine, sine)
    series = jnp.einsum('oxcn,cxbs->obsn', synthesis.astype(jnp.float32), rotated.astype(jnp.float32))
    return (visibilities, series)
```

```python
import functools
import math

import jax
import jax.numpy as jnp
import numpy as np
from jax import lax
from jax.experimental import pallas as pl
from jax.experimental.pallas import tpu as pltpu
from jax.sharding import PartitionSpec as P

POINTS = 256
TAPS = 8
ROWS = 16
STRETCH = 8
F32 = jnp.float32
BF16 = jnp.bfloat16
VMEM = 60 * 1024 * 1024


def fit_tables():
    spots = np.cos(np.pi * (np.arange(4000) + 0.5) / 4000) * 0.125 + 0.125
    powers = np.stack([spots ** (2 * k) for k in range(6)], 1)
    weight = np.ones_like(spots)
    sine = np.linalg.lstsq(powers[:, :5] * spots[:, None], np.sin(2 * np.pi * spots), rcond=None)[0]
    cosine = np.linalg.lstsq(powers, np.cos(2 * np.pi * spots) * weight, rcond=None)[0]
    return [float(v) for v in sine], [float(v) for v in cosine]


SINE_FIT, COSINE_FIT = fit_tables()


def prototype_taper(tap_count, point_count):
    spots = jnp.arange(tap_count * point_count, dtype=F32)
    length = float(tap_count * point_count)
    shaped = jnp.sinc((spots - length / 2.0 + 0.5) / point_count) * (
        0.5 - 0.5 * jnp.cos(2.0 * math.pi * (spots + 0.5) / length)
    )
    return shaped.reshape(tap_count, point_count)


def dft_tables(kept, point_count):
    spots = jnp.arange(point_count, dtype=jnp.int32)
    turns = kept[:, None] * spots[None, :] % point_count
    angle = turns.astype(F32) * (2.0 * math.pi / point_count)
    scale = 1.0 / math.sqrt(point_count)
    return jnp.cos(angle) * scale, jnp.sin(angle) * scale


def rotation(dm_rows, kept):
    squares = kept * kept % 4096
    turns = squares[:, None] * dm_rows[None, :] % 4096
    angle = turns.astype(F32) * (2.0 * math.pi / 4096.0)
    return (jnp.cos(angle), jnp.sin(angle))


def pieces(count, least):
    parts = min(least, count)
    edges = [count * k // parts for k in range(parts + 1)]
    return [(edges[k], edges[k + 1]) for k in range(parts)]


def spectra_kernel(counts, flags_ref, samples_ref, taper_ref, analysis_ref, *refs):
    out_refs, (frames_ref, wide_ref) = refs[: len(counts)], refs[len(counts) :]
    spectra_all = frames_ref.shape[1] // ROWS
    co_rows = analysis_ref.shape[0]

    def form_frames(step, carry):
        first = step * STRETCH
        for x in range(2):
            for half in range(POINTS // 128):
                lanes = pl.ds(half * 128, 128)
                tapers = [
                    jnp.broadcast_to(taper_ref[pl.ds(t, 1), lanes], (ROWS, 128)) for t in range(TAPS)
                ]
                tiles = []
                for k in range(STRETCH + TAPS - 1):
                    spot = pl.multiple_of((first + k) * POINTS + half * 128, 128)
                    tiles.append(samples_ref[x, :, pl.ds(spot, 128)].astype(F32))
                for s in range(STRETCH):
                    total = tiles[s] * tapers[0]
                    for t in range(1, TAPS):
                        total = total + tiles[s + t] * tapers[t]
                    row = pl.multiple_of((first + s) * ROWS, ROWS)
                    frames_ref[x * (POINTS // 128) + half, pl.ds(row, ROWS), :] = total
        return carry

    lax.fori_loop(0, spectra_all // STRETCH, form_frames, 0)

    group = pl.program_id(0)

    def transform(i, carry):
        frame = jnp.concatenate(
            [
                frames_ref[k, pl.ds(i, spectra_all, stride=ROWS), :].astype(BF16)
                for k in range(2 * POINTS // 128)
            ],
            axis=1,
        )
        product = lax.dot_general(
            analysis_ref[...], frame, (((1,), (1,)), ((), ())), preferred_element_type=F32
        )
        product = product * flags_ref[group * ROWS + i].astype(F32)
        for k in range(spectra_all // 128):
            wide_ref[k, pl.ds(i, co_rows, stride=ROWS), :] = product[:, k * 128 : (k + 1) * 128]
        return carry

    lax.fori_loop(0, ROWS, transform, 0)

    base = 0
    for count, out_ref in zip(counts, out_refs):
        gx_count = out_ref.shape[0]
        per = 2 * count

        def send_rows(d, carry, base=base, per=per, out_ref=out_ref):
            for k in range(per):
                row = pl.multiple_of((base + d * per + k) * ROWS, ROWS)
                for part in range(wide_ref.shape[0]):
                    out_ref[d, k // 2, k % 2, :, part * 128 : (part + 1) * 128] = wide_ref[
                        part, pl.ds(row, ROWS), :
                    ].astype(BF16)
            return carry

        lax.fori_loop(0, gx_count, send_rows, 0)
        base += gx_count * per


def spectra_of(samples, flags, taper, analysis, gx_count, counts, first, groups, spectra_all):
    co_rows = analysis.shape[0]
    return pl.pallas_call(
        functools.partial(spectra_kernel, counts),
        out_shape=[
            jax.ShapeDtypeStruct((gx_count, n, 2, groups * ROWS, spectra_all), BF16) for n in counts
        ],
        grid=(groups,),
        in_specs=[
            pl.BlockSpec(memory_space=pltpu.SMEM),
            pl.BlockSpec((2, ROWS, samples.shape[2]), lambda g: (0, g + first, 0)),
            pl.BlockSpec((TAPS, POINTS), lambda g: (0, 0)),
            pl.BlockSpec((co_rows, 2 * POINTS), lambda g: (0, 0)),
        ],
        out_specs=[
            pl.BlockSpec((gx_count, n, 2, ROWS, spectra_all), lambda g: (0, 0, 0, g, 0))
            for n in counts
        ],
        scratch_shapes=[
            pltpu.VMEM((2 * POINTS // 128, spectra_all * ROWS, 128), F32),
            pltpu.VMEM((spectra_all // 128, co_rows * ROWS, 128), F32),
        ],
        compiler_params=pltpu.CompilerParams(vmem_limit_bytes=VMEM),
        cost_estimate=pl.CostEstimate(
            flops=groups * ROWS * spectra_all * co_rows * 4 * POINTS,
            bytes_accessed=groups * ROWS * (samples.shape[2] * 4 + co_rows * spectra_all * 2),
            transcendentals=0,
        ),
        name="spectra",
    )(lax.dynamic_slice_in_dim(flags, first * ROWS, groups * ROWS), samples, taper, analysis)


def weights_kernel(kept_ref, delays_ref, out_ref):
    scale = kept_ref[pl.program_id(0)].astype(F32) * (1.0 / POINTS)
    input_scale = 1.0 / math.sqrt(delays_ref.shape[1])

    def rows(step, carry):
        at = pl.ds(pl.multiple_of(step * 16, 16), 16)
        turns = delays_ref[at, :] * scale
        turns = turns - jnp.floor(turns + 0.5)
        size = jnp.abs(turns)
        near = jnp.minimum(size, 0.5 - size)
        square = near * near
        sine = square * SINE_FIT[-1] + SINE_FIT[-2]
        for value in SINE_FIT[-3::-1]:
            sine = sine * square + value
        sine = sine * (near * input_scale)
        cosine = square * COSINE_FIT[-1] + COSINE_FIT[-2]
        for value in COSINE_FIT[-3::-1]:
            cosine = cosine * square + value
        cosine = cosine * input_scale
        out_ref[0, 0, at, :] = jnp.where(size > 0.25, -cosine, cosine).astype(BF16)
        out_ref[0, 1, at, :] = jnp.where(turns > 0.0, -sine, sine).astype(BF16)
        return carry

    lax.fori_loop(0, delays_ref.shape[0] // 16, rows, 0)


def weights_of(kept, delays):
    beams, inputs = delays.shape
    return pl.pallas_call(
        weights_kernel,
        out_shape=jax.ShapeDtypeStruct((kept.shape[0], 2, beams, inputs), BF16),
        grid=(kept.shape[0],),
        in_specs=[
            pl.BlockSpec(memory_space=pltpu.SMEM),
            pl.BlockSpec((beams, inputs), lambda c: (0, 0)),
        ],
        out_specs=pl.BlockSpec((1, 2, beams, inputs), lambda c: (c, 0, 0, 0)),
        compiler_params=pltpu.CompilerParams(vmem_limit_bytes=VMEM),
        cost_estimate=pl.CostEstimate(
            flops=kept.shape[0] * beams * inputs * 40,
            bytes_accessed=kept.shape[0] * beams * inputs * 4,
            transcendentals=0,
        ),
        name="weights",
    )(kept, delays)


def assemble(parts, joined_ref):
    span = sum(part.shape[3] for part in parts)
    for src in range(parts[0].shape[0]):
        at = src * span
        for part in parts:
            rows = part.shape[3]
            for o in range(2):
                joined_ref[o, at : at + rows, :] = part[src, 0, o]
            at += rows


def beams_kernel(part_count, *refs):
    parts, (weights_ref, turn_ref, out_ref, joined_ref) = refs[:part_count], refs[part_count:]
    assemble(parts, joined_ref)
    beams = weights_ref.shape[2]
    weights = weights_ref[0].reshape(2 * beams, weights_ref.shape[3])
    products = [
        jnp.dot(weights, joined_ref[o], preferred_element_type=F32) for o in range(2)
    ]
    real_part = (products[0][:beams] - products[1][beams:]).astype(BF16).astype(F32)
    imag_part = (products[1][:beams] + products[0][beams:]).astype(BF16).astype(F32)
    cosine, sine = turn_ref[0, :, 0:1], turn_ref[0, :, 1:2]
    first = (real_part * cosine + imag_part * sine).astype(BF16)
    second = (imag_part * cosine - real_part * sine).astype(BF16)
    if len(out_ref.shape) == 5:
        out_ref[:, 0, 0] = first.reshape(out_ref.shape[0], out_ref.shape[3], out_ref.shape[4])
        out_ref[:, 0, 1] = second.reshape(out_ref.shape[0], out_ref.shape[3], out_ref.shape[4])
    else:
        out_ref[0, 0] = first
        out_ref[0, 1] = second


def part_specs(arrays, firsts):
    return [
        pl.BlockSpec(
            (a.shape[0], 1, 2, a.shape[3], a.shape[4]),
            functools.partial(lambda c, first: (0, c + first, 0, 0, 0), first=first),
        )
        for a, first in zip(arrays, firsts)
    ]


def beams_of(arrays, firsts, weights, turns, first, count, gx_count):
    beams, inputs = weights.shape[2:]
    spectra_all = arrays[0].shape[4]
    beam_dev = beams // gx_count
    if beam_dev % 16 == 0:
        out_shape = (gx_count, count, 2, beam_dev, spectra_all)
        out_spec = pl.BlockSpec((gx_count, 1, 2, beam_dev, spectra_all), lambda c: (0, c, 0, 0, 0))
    else:
        out_shape = (count, 2, beams, spectra_all)
        out_spec = pl.BlockSpec((1, 2, beams, spectra_all), lambda c: (c, 0, 0, 0))
    out = pl.pallas_call(
        functools.partial(beams_kernel, len(arrays)),
        out_shape=jax.ShapeDtypeStruct(out_shape, BF16),
        grid=(count,),
        in_specs=part_specs(arrays, firsts)
        + [
            pl.BlockSpec((1, 2, beams, inputs), lambda c: (c + first, 0, 0, 0)),
            pl.BlockSpec((1, beams, 2), lambda c: (c + first, 0, 0)),
        ],
        out_specs=out_spec,
        scratch_shapes=[pltpu.VMEM((2, inputs, spectra_all), BF16)],
        compiler_params=pltpu.CompilerParams(vmem_limit_bytes=VMEM),
        cost_estimate=pl.CostEstimate(
            flops=count * beams * inputs * spectra_all * 8,
            bytes_accessed=count * inputs * (spectra_all * 4 + beams * 4),
            transcendentals=0,
        ),
        name="beams",
    )(*arrays, weights, turns)
    if beam_dev % 16:
        out = out.reshape(count, 2, gx_count, beam_dev, spectra_all).transpose(2, 0, 1, 3, 4)
    return out


def gram_kernel(part_count, *refs):
    parts, (out_ref, joined_ref) = refs[:part_count], refs[-2:]
    assemble(parts, joined_ref)
    inputs, spectra_all = joined_ref.shape[1:]
    side = 256
    scale = 1.0 / spectra_all
    contract = (((1,), (1,)), ((), ()))

    def product(left, right, rows, columns):
        return lax.dot_general(
            joined_ref[left, rows], joined_ref[right, columns], contract, preferred_element_type=F32
        )

    for j in range(inputs // side):
        columns = slice(j * side, (j + 1) * side)
        above = slice(0, (j + 1) * side)
        below = slice(j * side, inputs)
        real_sum = product(0, 0, above, columns) + product(1, 1, above, columns)
        mixed = product(1, 0, below, columns) - product(0, 1, below, columns)
        if j:
            out_ref[0, : j * side, columns] = (real_sum[: j * side] * scale).astype(BF16)
        upper = lax.broadcasted_iota(jnp.int32, (side, side), 0) <= lax.broadcasted_iota(
            jnp.int32, (side, side), 1
        )
        out_ref[0, columns, columns] = (
            jnp.where(upper, real_sum[j * side :], mixed[:side]) * scale
        ).astype(BF16)
        if (j + 1) * side < inputs:
            out_ref[0, (j + 1) * side :, columns] = (mixed[side:] * scale).astype(BF16)


def gram_of(arrays, firsts, first, count, channels, held):
    spectra_all = arrays[0].shape[4]
    inputs = arrays[0].shape[0] * sum(a.shape[3] for a in arrays)
    more = [] if held is None else [held]
    return pl.pallas_call(
        functools.partial(gram_kernel, len(arrays)),
        out_shape=jax.ShapeDtypeStruct((channels, inputs, inputs), BF16),
        grid=(count,),
        in_specs=part_specs(arrays, firsts) + [pl.BlockSpec(memory_space=pl.ANY)] * len(more),
        out_specs=pl.BlockSpec((1, inputs, inputs), lambda c: (c + first, 0, 0)),
        scratch_shapes=[pltpu.VMEM((2, inputs, spectra_all), BF16)],
        input_output_aliases={len(arrays): 0} if more else {},
        compiler_params=pltpu.CompilerParams(vmem_limit_bytes=VMEM),
        cost_estimate=pl.CostEstimate(
            flops=count * inputs * inputs * spectra_all * 5,
            bytes_accessed=count * inputs * (spectra_all * 4 + inputs * 2),
            transcendentals=0,
        ),
        name="gram",
    )(*arrays, *more)


def series_kernel(part_count, *refs):
    parts, (synthesis_ref, out_ref, wide_ref) = refs[:part_count], refs[part_count:]
    beam = pl.program_id(0)
    beam_dev, spectra_all = parts[0].shape[3:]
    rows = synthesis_ref.shape[0]

    @pl.when(beam == 0)
    def _():
        base = 0
        for part in parts:
            sources, count = part.shape[:2]

            def widen(d, carry, base=base, part=part, count=count):
                for k in range(2 * count):
                    row = pl.multiple_of((base + d * 2 * count + k) * beam_dev, beam_dev)
                    for half in range(spectra_all // 128):
                        wide_ref[half, pl.ds(row, beam_dev), :] = part[
                            d, k // 2, k % 2, :, half * 128 : (half + 1) * 128
                        ].astype(F32)
                return carry

            lax.fori_loop(0, sources, widen, 0)
            base += sources * count * 2

    turned = jnp.concatenate(
        [
            wide_ref[k, pl.ds(beam, rows, stride=beam_dev), :].astype(BF16)
            for k in range(spectra_all // 128)
        ],
        axis=1,
    )
    product = lax.dot_general(
        turned, synthesis_ref[...], (((0,), (0,)), ((), ())), preferred_element_type=F32
    )
    for o in range(2):
        out_ref[o, 0] = product[:, o * POINTS : (o + 1) * POINTS]


def series_of(arrays, synthesis):
    gx_count, _, _, beam_dev, spectra_all = arrays[0].shape
    rows = synthesis.shape[0]
    return pl.pallas_call(
        functools.partial(series_kernel, len(arrays)),
        out_shape=jax.ShapeDtypeStruct((2, beam_dev, spectra_all, POINTS), F32),
        grid=(beam_dev,),
        in_specs=[pl.BlockSpec(a.shape, lambda b: (0, 0, 0, 0, 0)) for a in arrays]
        + [pl.BlockSpec(synthesis.shape, lambda b: (0, 0))],
        out_specs=pl.BlockSpec((2, 1, spectra_all, POINTS), lambda b: (0, b, 0, 0)),
        scratch_shapes=[pltpu.VMEM((spectra_all // 128, rows * beam_dev, 128), F32)],
        compiler_params=pltpu.CompilerParams(vmem_limit_bytes=VMEM),
        cost_estimate=pl.CostEstimate(
            flops=2 * beam_dev * rows * spectra_all * 2 * POINTS,
            bytes_accessed=beam_dev * spectra_all * (rows * 2 + POINTS * 8),
            transcendentals=0,
        ),
        name="series",
    )(*arrays, synthesis)


def exchange(array):
    return lax.all_to_all(array, "gx", split_axis=0, concat_axis=0, tiled=True)


def shards(samples, flags, kept_channels, beam_order, dm_bins, delays):
    gx_count = lax.axis_size("gx")
    my_index = lax.axis_index("gx")
    channels = kept_channels.shape[0]
    chan_dev = channels // gx_count
    spectra_all = samples.shape[2] // POINTS - TAPS + 1
    groups = samples.shape[1] // ROWS

    taper = prototype_taper(TAPS, POINTS)
    cosine, sine = dft_tables(kept_channels, POINTS)
    table = jnp.stack(
        [jnp.concatenate([cosine, sine], 1), jnp.concatenate([-sine, cosine], 1)], 1
    ).astype(BF16)
    by_owner = jnp.reshape(table, (gx_count, chan_dev, 2, 2 * POINTS))
    chunks = pieces(chan_dev, 3)

    def ordered(table, cuts):
        return jnp.concatenate(
            [table[:, a:b].reshape(-1, 2 * POINTS) for a, b in cuts], 0
        )

    lead = 1 if groups > 1 else 0
    parts = []
    if lead:
        (head,) = spectra_of(
            samples, flags, taper, ordered(by_owner, [(0, chan_dev)]), gx_count, [chan_dev], 0, 1,
            spectra_all,
        )
        head = exchange(head)
    rest = spectra_of(
        samples, flags, taper, ordered(by_owner, chunks), gx_count, [b - a for a, b in chunks],
        lead, groups - lead, spectra_all,
    )
    rest = [exchange(r) for r in rest]

    my_kept = lax.dynamic_slice_in_dim(kept_channels, my_index * chan_dev, chan_dev)
    weights = weights_of(my_kept, jnp.take(delays, beam_order, axis=0))
    turns = jnp.stack(rotation(jnp.take(dm_bins, beam_order), my_kept), 2)

    visibilities = None
    sums = []
    for (a, b), block in zip(chunks, rest):
        arrays, firsts = ([head, block], [a, 0]) if lead else ([block], [0])
        sums.append(exchange(beams_of(arrays, firsts, weights, turns, a, b - a, gx_count)))
        visibilities = gram_of(arrays, firsts, a, b - a, chan_dev, visibilities)
    series = series_of(
        sums, ordered(by_owner, chunks)
    )
    return (visibilities, series)


def solution(mesh):
    placed = (P(None, ("groups", "gx"), None), P("gx"), P(), P(), P("groups"), P("groups", None))
    return jax.shard_map(
        shards,
        mesh=mesh,
        in_specs=placed,
        out_specs=(P(("groups", "gx"), None, None), P(None, ("groups", "gx"), None, None)),
        check_vma=False,
    )
```

```python
import functools
import math

import jax
import jax.numpy as jnp
import numpy as np
from jax import lax
from jax.experimental import pallas as pl
from jax.experimental.pallas import tpu as pltpu
from jax.sharding import PartitionSpec as P

POINTS = 256
TAPS = 8
ROWS = 16
EACH = 3
SHARE = 4
APART = 12
LEAD = 1
STRETCH = 16
F32 = jnp.float32
BF16 = jnp.bfloat16
VMEM = 60 * 1024 * 1024
BEAMS_VMEM = VMEM


def fit_tables():
    spots = np.cos(np.pi * (np.arange(4000) + 0.5) / 4000) * 0.125 + 0.125
    powers = np.stack([spots ** (2 * k) for k in range(6)], 1)
    sine = np.linalg.lstsq(powers[:, :5] * spots[:, None], np.sin(2 * np.pi * spots), rcond=None)[0]
    cosine = np.linalg.lstsq(powers, np.cos(2 * np.pi * spots), rcond=None)[0]
    return [float(v) for v in sine], [float(v) for v in cosine]


SINE_FIT, COSINE_FIT = fit_tables()


def prototype_taper(tap_count, point_count):
    spots = np.arange(tap_count * point_count, dtype=np.float64)
    length = float(tap_count * point_count)
    shaped = np.sinc((spots - length / 2.0 + 0.5) / point_count) * (
        0.5 - 0.5 * np.cos(2.0 * math.pi * (spots + 0.5) / length)
    )
    return shaped.reshape(tap_count, point_count).astype(np.float32)


def dft_tables(kept, point_count):
    spots = jnp.arange(point_count, dtype=jnp.int32)
    turns = kept[:, None] * spots[None, :] % point_count
    angle = turns.astype(F32) * (2.0 * math.pi / point_count)
    scale = 1.0 / math.sqrt(point_count)
    return jnp.cos(angle) * scale, jnp.sin(angle) * scale


def rotation(dm_rows, kept):
    squares = kept * kept % 4096
    turns = squares[:, None] * dm_rows[None, :] % 4096
    angle = turns.astype(F32) * (2.0 * math.pi / 4096.0)
    return (jnp.cos(angle), jnp.sin(angle))


def spectra_kernel(first, counts, *refs):
    me_ref, flags_ref, samples_ref, taper_ref, analysis_ref = refs[:5]
    out_refs, (frames_ref, wide_ref) = refs[5:-2], refs[-2:]
    span = frames_ref.shape[1] // ROWS
    co_rows = analysis_ref.shape[0]
    step = pl.program_id(0) + first
    group, begin = step // 2, (step % 2) * span

    def form_frames(stretch, carry):
        at = stretch * STRETCH
        for x in range(2):
            for half in range(POINTS // 128):
                lanes = pl.ds(half * 128, 128)
                tapers = [
                    jnp.broadcast_to(taper_ref[pl.ds(t, 1), lanes], (ROWS, 128)) for t in range(TAPS)
                ]
                tiles = []
                for k in range(STRETCH + TAPS - 1):
                    spot = pl.multiple_of((begin + at + k) * POINTS + half * 128, 128)
                    tiles.append(samples_ref[x, :, pl.ds(spot, 128)].astype(F32))
                for s in range(STRETCH):
                    total = tiles[s] * tapers[0]
                    for t in range(1, TAPS):
                        total = total + tiles[s + t] * tapers[t]
                    row = pl.multiple_of((at + s) * ROWS, ROWS)
                    frames_ref[x * (POINTS // 128) + half, pl.ds(row, ROWS), :] = total
        return carry

    lax.fori_loop(0, span // STRETCH, form_frames, 0)

    def transform(pair, carry):
        frame = jnp.concatenate(
            [
                jnp.concatenate(
                    [
                        frames_ref[k, pl.ds(2 * pair + i, span, stride=ROWS), :].astype(BF16)
                        for k in range(2 * POINTS // 128)
                    ],
                    axis=1,
                )
                for i in range(2)
            ],
            axis=0,
        )
        product = lax.dot_general(
            analysis_ref[...], frame, (((1,), (1,)), ((), ())), preferred_element_type=F32
        )
        for i in range(2):
            gain = flags_ref[group * ROWS + 2 * pair + i].astype(F32)
            wide_ref[pl.ds(2 * pair + i, co_rows, stride=ROWS), :] = (
                product[:, i * span : (i + 1) * span] * gain
            )
        return carry

    lax.fori_loop(0, ROWS // 2, transform, 0, unroll=4)

    def send(out, place, row):
        out[place] = wide_ref[pl.ds(pl.multiple_of(row * ROWS, ROWS), ROWS), :].astype(BF16)

    count, gx_count = counts[0], out_refs[0].shape[0]

    chan_dev = count + counts[1]

    def send_rows(d, carry):
        for k in range(2 * count):
            send(out_refs[0], (d, k // 2, k % 2), d * 2 * chan_dev + k)
        return carry

    lax.fori_loop(0, gx_count, send_rows, 0)
    for k, out in enumerate(out_refs[1:]):
        for slot in range(2):
            owner = me_ref[0] ^ k ^ (slot * (gx_count // 2))
            for j in range(2 * counts[1]):
                send(out, (slot, j // 2, j % 2), (owner * chan_dev + count) * 2 + j)


def spectra_of(samples, flags, me, taper, analysis, gx_count, counts, first, steps, span):
    co_rows = analysis.shape[0]
    rows = steps * ROWS
    out_shape = [jax.ShapeDtypeStruct((gx_count, counts[0], 2, rows, span), BF16)]
    out_specs = [pl.BlockSpec((gx_count, counts[0], 2, ROWS, span), lambda g: (0, 0, 0, g, 0))]
    if counts[1]:
        half = gx_count // 2
        shape = (2, counts[1], 2, rows, span)
        out_shape += [jax.ShapeDtypeStruct(shape, BF16)] * half
        out_specs += [pl.BlockSpec((2, counts[1], 2, ROWS, span), lambda g: (0, 0, 0, g, 0))] * half
    width = samples.shape[2] if steps > 1 or first else (span + TAPS - 1) * POINTS
    return pl.pallas_call(
        functools.partial(spectra_kernel, first, counts),
        out_shape=out_shape,
        grid=(steps,),
        in_specs=[
            pl.BlockSpec(memory_space=pltpu.SMEM),
            pl.BlockSpec(memory_space=pltpu.SMEM),
            pl.BlockSpec((2, ROWS, width), lambda g: (0, (g + first) // 2, 0)),
            pl.BlockSpec((TAPS, POINTS), lambda g: (0, 0)),
            pl.BlockSpec((co_rows, 2 * POINTS), lambda g: (0, 0)),
        ],
        out_specs=out_specs,
        scratch_shapes=[
            pltpu.VMEM((2 * POINTS // 128, span * ROWS, 128), F32),
            pltpu.VMEM((co_rows * ROWS, span), F32),
        ],
        compiler_params=pltpu.CompilerParams(vmem_limit_bytes=VMEM),
        cost_estimate=pl.CostEstimate(
            flops=steps * ROWS * span * co_rows * 4 * POINTS * 3,
            bytes_accessed=steps * ROWS * (samples.shape[2] * 4 + co_rows * span * 2),
            transcendentals=0,
        ),
        name="spectra",
    )(me, flags, samples, taper, analysis)


def weights_kernel(kept_ref, delays_ref, out_ref):
    scale = kept_ref[pl.program_id(0)].astype(F32) * (1.0 / POINTS)
    input_scale = 1.0 / math.sqrt(delays_ref.shape[1])

    def rows(step, carry):
        at = pl.ds(pl.multiple_of(step * 16, 16), 16)
        turns = delays_ref[at, :] * scale
        turns = turns - jnp.floor(turns + 0.5)
        size = jnp.abs(turns)
        near = jnp.minimum(size, 0.5 - size)
        square = near * near
        sine = square * SINE_FIT[-1] + SINE_FIT[-2]
        for value in SINE_FIT[-3::-1]:
            sine = sine * square + value
        sine = sine * (near * input_scale)
        cosine = square * COSINE_FIT[-1] + COSINE_FIT[-2]
        for value in COSINE_FIT[-3::-1]:
            cosine = cosine * square + value
        cosine = cosine * input_scale
        out_ref[0, 0, at, :] = jnp.where(size > 0.25, -cosine, cosine).astype(BF16)
        out_ref[0, 1, at, :] = jnp.where(turns > 0.0, -sine, sine).astype(BF16)
        return carry

    lax.fori_loop(0, delays_ref.shape[0] // 16, rows, 0)


def weights_of(kept, delays):
    beams, inputs = delays.shape
    return pl.pallas_call(
        weights_kernel,
        out_shape=jax.ShapeDtypeStruct((kept.shape[0], 2, beams, inputs), BF16),
        grid=(kept.shape[0],),
        in_specs=[
            pl.BlockSpec(memory_space=pltpu.SMEM),
            pl.BlockSpec((beams, inputs), lambda c: (0, 0)),
        ],
        out_specs=pl.BlockSpec((1, 2, beams, inputs), lambda c: (c, 0, 0, 0)),
        compiler_params=pltpu.CompilerParams(vmem_limit_bytes=VMEM),
        cost_estimate=pl.CostEstimate(
            flops=kept.shape[0] * beams * inputs * 40,
            bytes_accessed=kept.shape[0] * beams * inputs * 4,
            transcendentals=0,
        ),
        name="weights",
    )(kept, delays)


def assemble(me_ref, lead, rest, c, joined_ref):
    sources, _, _, lead_rows, span = lead.shape
    ahead = lead_rows // ROWS
    steps = rest[-1].shape[-2] // ROWS + ahead
    share = steps // 2 * ROWS
    half = sources // 2

    def place(src, o, step, block):
        row = src * share + step // 2 * ROWS
        if not isinstance(row, int):
            row = pl.multiple_of(row, ROWS)
        joined_ref[o, pl.ds(row, ROWS), pl.ds(step % 2 * span, span)] = block

    for k in range(sources):
        for o in range(2):
            for step in range(ahead):
                place(k, o, step, lead[k, c, o, pl.ds(step * ROWS, ROWS), :])
            for step in range(ahead, steps):
                rows = pl.ds((step - ahead) * ROWS, ROWS)
                if len(rest) == 1:
                    place(k, o, step, rest[0][k, c, o, rows, :])
                elif k < half:
                    place(me_ref[0] ^ k, o, step, rest[k][0, c, o, rows, :])
                else:
                    place(me_ref[0] ^ k, o, step, rest[half][k - half, c, o, rows, :])


def beams_kernel(part_count, me_ref, lead, *refs):
    rest, (weights_ref, turn_ref) = refs[:part_count], refs[part_count : part_count + 2]
    each, _, beams, inputs = weights_ref.shape
    out_ref, joined_refs = refs[-1 - each], refs[-each:]
    for c in range(each):
        assemble(me_ref, lead, rest, c, joined_refs[c])
        weights = weights_ref[c].reshape(2 * beams, inputs)
        products = [jnp.dot(weights, joined_refs[c][o], preferred_element_type=F32) for o in range(2)]
        real_part = (products[0][:beams] - products[1][beams:]).astype(BF16).astype(F32)
        imag_part = (products[1][:beams] + products[0][beams:]).astype(BF16).astype(F32)
        cosine, sine = turn_ref[c, :, 0:1], turn_ref[c, :, 1:2]
        turned = [
            (real_part * cosine + imag_part * sine).astype(BF16),
            (imag_part * cosine - real_part * sine).astype(BF16),
        ]
        for x in range(2):
            if len(out_ref.shape) == 5:
                shape = (out_ref.shape[0],) + out_ref.shape[3:]
                out_ref[:, c, x] = turned[x].reshape(shape)
            else:
                out_ref[c, x] = turned[x]


def part_specs(lead, rest, first, at, each):
    specs = [
        pl.BlockSpec(memory_space=pltpu.SMEM),
        pl.BlockSpec((lead.shape[0], each) + lead.shape[2:], lambda c: (0, c + first // each, 0, 0, 0)),
    ]
    for a in rest[:-1]:
        specs.append(pl.BlockSpec((1, each) + a.shape[2:], lambda c: (0, c + at // each, 0, 0, 0)))
    far = rest[-1]
    specs.append(pl.BlockSpec((far.shape[0], each) + far.shape[2:], lambda c: (0, c, 0, 0, 0)))
    return specs


def beams_of(me, lead, rest, weights, turns, first, at, count, held):
    channels, _, beams, inputs = weights.shape
    gx_count, span = lead.shape[0], lead.shape[4]
    spectra_all = 2 * span
    beam_dev = beams // gx_count
    each = EACH if count % EACH == 0 and first % EACH == 0 and at % EACH == 0 else 1
    start = first // each
    if beam_dev % 16 == 0:
        out_shape = (gx_count, channels, 2, beam_dev, spectra_all)
        out_spec = pl.BlockSpec(
            (gx_count, each, 2, beam_dev, spectra_all), lambda c: (0, c + start, 0, 0, 0)
        )
    else:
        out_shape = (channels, 2, beams, spectra_all)
        out_spec = pl.BlockSpec((each, 2, beams, spectra_all), lambda c: (c + start, 0, 0, 0))
    more = [] if held is None else [held]
    return pl.pallas_call(
        functools.partial(beams_kernel, len(rest)),
        out_shape=jax.ShapeDtypeStruct(out_shape, BF16),
        grid=(count // each,),
        in_specs=part_specs(lead, rest, first, at, each)
        + [
            pl.BlockSpec((each, 2, beams, inputs), lambda c: (c + start, 0, 0, 0)),
            pl.BlockSpec((each, beams, 2), lambda c: (c + start, 0, 0)),
        ]
        + [pl.BlockSpec(memory_space=pl.ANY)] * len(more),
        out_specs=out_spec,
        scratch_shapes=[pltpu.VMEM((2, inputs, spectra_all), BF16)] * each,
        input_output_aliases={4 + len(rest): 0} if more else {},
        compiler_params=pltpu.CompilerParams(vmem_limit_bytes=BEAMS_VMEM),
        cost_estimate=pl.CostEstimate(
            flops=count * beams * inputs * spectra_all * 8,
            bytes_accessed=count * inputs * (spectra_all * 4 + beams * 4),
            transcendentals=0,
        ),
        name="beams",
    )(me, lead, *rest, weights, turns, *more)


def gram_kernel(part_count, me_ref, lead, *refs):
    (out_ref, joined_ref) = refs[-2:]
    rest = refs[:part_count]
    assemble(me_ref, lead, rest, 0, joined_ref)
    inputs, spectra_all = joined_ref.shape[1:]
    side = 256
    scale = 1.0 / spectra_all
    contract = (((1,), (1,)), ((), ()))

    def product(left, right, rows, columns):
        return lax.dot_general(
            joined_ref[left, rows], joined_ref[right, columns], contract, preferred_element_type=F32
        )

    for j in range(inputs // side):
        columns = slice(j * side, (j + 1) * side)
        above = slice(0, (j + 1) * side)
        below = slice(j * side, inputs)
        real_sum = product(0, 0, above, columns) + product(1, 1, above, columns)
        mixed = product(1, 0, below, columns) - product(0, 1, below, columns)
        if j:
            out_ref[0, : j * side, columns] = (real_sum[: j * side] * scale).astype(BF16)
        upper = lax.broadcasted_iota(jnp.int32, (side, side), 0) <= lax.broadcasted_iota(
            jnp.int32, (side, side), 1
        )
        out_ref[0, columns, columns] = (
            jnp.where(upper, real_sum[j * side :], mixed[:side]) * scale
        ).astype(BF16)
        if (j + 1) * side < inputs:
            out_ref[0, (j + 1) * side :, columns] = (mixed[side:] * scale).astype(BF16)


def gram_of(me, lead, rest, first, at, count, held):
    sources, channels, _, _, span = lead.shape
    inputs = sources * (rest[-1].shape[-2] + lead.shape[3]) // 2
    more = [] if held is None else [held]
    return pl.pallas_call(
        functools.partial(gram_kernel, len(rest)),
        out_shape=jax.ShapeDtypeStruct((channels, inputs, inputs), BF16),
        grid=(count,),
        in_specs=part_specs(lead, rest, first, at, 1) + [pl.BlockSpec(memory_space=pl.ANY)] * len(more),
        out_specs=pl.BlockSpec((1, inputs, inputs), lambda c: (c + first, 0, 0)),
        scratch_shapes=[pltpu.VMEM((2, inputs, 2 * span), BF16)],
        input_output_aliases={2 + len(rest): 0} if more else {},
        compiler_params=pltpu.CompilerParams(vmem_limit_bytes=VMEM),
        cost_estimate=pl.CostEstimate(
            flops=count * inputs * inputs * span * 10,
            bytes_accessed=count * inputs * (span * 8 + inputs * 2),
            transcendentals=0,
        ),
        name="gram",
    )(me, lead, *rest, *more)


def series_kernel(share, part_count, *refs):
    parts, (synthesis_ref, out_ref, wide_ref) = refs[:part_count], refs[part_count:]
    beam_dev, spectra_all = parts[0].shape[3:]
    rows = synthesis_ref.shape[0]
    halves = [slice(k * 128, (k + 1) * 128) for k in range(spectra_all // 128)]

    @pl.when(pl.program_id(0) == 0)
    def _():
        base = 0
        for part in parts:
            each = 2 * part.shape[1]

            def widen_source(d, carry, base=base, part=part, each=each):
                for j in range(each):
                    block = part[d, j // 2, j % 2]
                    row = pl.multiple_of((base + d * each + j) * beam_dev, beam_dev)
                    for k, half in enumerate(halves):
                        wide_ref[k, pl.ds(row, beam_dev), :] = block[:, half].astype(F32)
                return carry

            lax.fori_loop(0, part.shape[0], widen_source, 0)
            base += part.shape[0] * each

    for b in range(share):
        beam = pl.program_id(0) * share + b
        turned = jnp.concatenate(
            [
                wide_ref[k, pl.ds(beam, rows, stride=beam_dev), :].astype(BF16)
                for k in range(len(halves))
            ],
            axis=1,
        )
        product = lax.dot_general(
            turned, synthesis_ref[...], (((0,), (0,)), ((), ())), preferred_element_type=F32
        )
        for o in range(2):
            out_ref[o, b] = product[:, o * POINTS : (o + 1) * POINTS]


def series_of(parts, synthesis):
    beam_dev, spectra_all = parts[0].shape[3:]
    rows = synthesis.shape[0]
    share = SHARE
    return pl.pallas_call(
        functools.partial(series_kernel, share, len(parts)),
        out_shape=jax.ShapeDtypeStruct((2, beam_dev, spectra_all, POINTS), F32),
        grid=(beam_dev // share,),
        in_specs=[pl.BlockSpec(a.shape, lambda b: (0, 0, 0, 0, 0)) for a in parts]
        + [pl.BlockSpec(synthesis.shape, lambda b: (0, 0))],
        out_specs=pl.BlockSpec((2, share, spectra_all, POINTS), lambda b: (0, b, 0, 0)),
        scratch_shapes=[pltpu.VMEM((spectra_all // 128, rows * beam_dev, 128), F32)],
        compiler_params=pltpu.CompilerParams(vmem_limit_bytes=VMEM),
        cost_estimate=pl.CostEstimate(
            flops=2 * beam_dev * rows * spectra_all * 2 * POINTS,
            bytes_accessed=beam_dev * spectra_all * (rows * 2 + POINTS * 8),
            transcendentals=0,
        ),
        name="series",
    )(*parts, synthesis)


def exchange(array):
    return lax.all_to_all(array, "gx", split_axis=0, concat_axis=0, tiled=True)


tie = lax.optimization_barrier


def swap(array, k, count):
    return lax.ppermute(array, "gx", [(i, i ^ k) for i in range(count)])


def shards(samples, flags, kept_channels, beam_order, dm_bins, delays):
    gx_count = lax.axis_size("gx")
    me = lax.axis_index("gx").astype(jnp.int32)
    channels = kept_channels.shape[0]
    chan_dev = channels // gx_count
    span = (samples.shape[2] // POINTS - TAPS + 1) // 2
    steps = samples.shape[1] // ROWS * 2
    ahead = min(LEAD, steps // 2)
    apart = chan_dev // APART if gx_count <= 16 and gx_count & (gx_count - 1) == 0 else 0
    main = chan_dev - apart
    spot = me.reshape(1)

    taper = jnp.asarray(prototype_taper(TAPS, POINTS))
    cosine, sine = dft_tables(kept_channels, POINTS)
    table = jnp.stack(
        [jnp.concatenate([cosine, sine], 1), jnp.concatenate([-sine, cosine], 1)], 1
    ).astype(BF16)
    table_rows = table.reshape(-1, 2 * POINTS)
    (lead,) = spectra_of(
        samples, flags, spot, taper, table_rows, gx_count, (chan_dev, 0), 0, ahead, span
    )
    spot, lead = tie((spot, lead))
    rest, *near = spectra_of(
        samples, flags, spot, taper, table_rows, gx_count, (main, apart), ahead, steps - ahead, span
    )
    lead = exchange(lead)
    my_kept = lax.dynamic_slice_in_dim(kept_channels, me * chan_dev, chan_dev)
    my_kept, rest = tie((my_kept, rest))
    weights = weights_of(my_kept, jnp.take(delays, beam_order, axis=0))
    turns = jnp.stack(rotation(jnp.take(dm_bins, beam_order), my_kept), 2)

    half = gx_count // 2
    cuts = [(0, apart - 1), (apart - 1, apart)] if apart > 1 else [(0, apart)] * (apart > 0)
    relays = []
    if apart:
        near = near[:1] + [swap(near[k], k, gx_count) for k in range(1, half)]
        relays = [jnp.stack([n[1, a:b] for n in near], 0) for a, b in cuts]
    rest, lead = tie((rest, lead))
    rest = exchange(rest)

    beams, visibilities = None, None
    for order, (a, b) in enumerate(cuts):
        if order == len(cuts) - 1:
            if order:
                rest, relays, beams, visibilities = tie((rest, relays, beams, visibilities))
            else:
                rest, relays = tie((rest, relays))
            far = swap(relays[order], half, gx_count)
            beams = beams_of(spot, lead, [rest], weights, turns, 0, 0, main, beams)
        else:
            far = swap(relays[order], half, gx_count)
        parts = near + [far]
        beams = beams_of(spot, lead, parts, weights, turns, main + a, a, b - a, beams)
        if order < len(cuts) - 1:
            visibilities = gram_of(spot, lead, parts, main + a, a, b - a, visibilities)
    if not cuts:
        beams = beams_of(spot, lead, [rest], weights, turns, 0, 0, main, beams)
    spot, beams = tie((spot, beams))
    if beams.ndim == 4:
        beams = beams.reshape(chan_dev, 2, gx_count, -1, beams.shape[3]).transpose(2, 0, 1, 3, 4)
    sums = exchange(beams)
    visibilities = gram_of(spot, lead, [rest], 0, 0, main, visibilities)
    for a, b in cuts[-1:]:
        visibilities = gram_of(spot, lead, parts, main + a, a, b - a, visibilities)
    series = series_of([sums], table_rows)
    return (visibilities, series)


def solution(mesh):
    placed = (P(None, ("groups", "gx"), None), P("gx"), P(), P(), P("groups"), P("groups", None))
    return jax.shard_map(
        shards,
        mesh=mesh,
        in_specs=placed,
        out_specs=(P(("groups", "gx"), None, None), P(None, ("groups", "gx"), None, None)),
        check_vma=False,
    )
```

```python
import functools
import math

import jax
import jax.numpy as jnp
import numpy as np
from jax import lax
from jax.experimental import pallas as pl
from jax.experimental.pallas import tpu as pltpu
from jax.sharding import PartitionSpec as P

POINTS = 256
TAPS = 8
ROWS = 16
EACH = 3
SHARE = 8
APART = 12
LEAD = 1
PITCH = 24
STRETCH = 16
F32 = jnp.float32
BF16 = jnp.bfloat16
VMEM = 60 * 1024 * 1024
BEAMS_VMEM = VMEM


def fit_tables():
    spots = np.cos(np.pi * (np.arange(4000) + 0.5) / 4000) * 0.125 + 0.125
    powers = np.stack([spots ** (2 * k) for k in range(6)], 1)
    sine = np.linalg.lstsq(powers[:, :5] * spots[:, None], np.sin(2 * np.pi * spots), rcond=None)[0]
    cosine = np.linalg.lstsq(powers, np.cos(2 * np.pi * spots), rcond=None)[0]
    return [float(v) for v in sine], [float(v) for v in cosine]


SINE_FIT, COSINE_FIT = fit_tables()


def prototype_taper(tap_count, point_count):
    spots = np.arange(tap_count * point_count, dtype=np.float64)
    length = float(tap_count * point_count)
    shaped = np.sinc((spots - length / 2.0 + 0.5) / point_count) * (
        0.5 - 0.5 * np.cos(2.0 * math.pi * (spots + 0.5) / length)
    )
    return shaped.reshape(tap_count, point_count).astype(np.float32)


def dft_tables(kept, point_count):
    spots = jnp.arange(point_count, dtype=jnp.int32)
    turns = kept[:, None] * spots[None, :] % point_count
    angle = turns.astype(F32) * (2.0 * math.pi / point_count)
    scale = 1.0 / math.sqrt(point_count)
    return jnp.cos(angle) * scale, jnp.sin(angle) * scale


def rotation(dm_rows, kept):
    squares = kept * kept % 4096
    turns = squares[:, None] * dm_rows[None, :] % 4096
    angle = turns.astype(F32) * (2.0 * math.pi / 4096.0)
    return (jnp.cos(angle), jnp.sin(angle))


def spectra_kernel(first, counts, *refs):
    me_ref, flags_ref, samples_ref, taper_ref, analysis_ref = refs[:5]
    out_refs, (frames_ref, wide_ref) = refs[5:-2], refs[-2:]
    span = frames_ref.shape[1] // PITCH
    co_rows = analysis_ref.shape[0]
    step = pl.program_id(0) + first
    group, begin = step // 2, (step % 2) * span

    def form_frames(stretch, carry):
        at = stretch * STRETCH
        for x in range(2):
            for half in range(POINTS // 128):
                lanes = pl.ds(half * 128, 128)
                tapers = [
                    jnp.broadcast_to(taper_ref[pl.ds(t, 1), lanes], (ROWS, 128)) for t in range(TAPS)
                ]
                tiles = []
                for k in range(STRETCH + TAPS - 1):
                    spot = pl.multiple_of((begin + at + k) * POINTS + half * 128, 128)
                    tiles.append(samples_ref[x, :, pl.ds(spot, 128)].astype(F32))
                for s in range(STRETCH):
                    total = tiles[s] * tapers[0]
                    for t in range(1, TAPS):
                        total = total + tiles[s + t] * tapers[t]
                    row = pl.multiple_of((at + s) * PITCH, 8)
                    frames_ref[x * (POINTS // 128) + half, pl.ds(row, ROWS), :] = total
        return carry

    lax.fori_loop(0, span // STRETCH, form_frames, 0)

    def transform(pair, carry):
        frame = jnp.concatenate(
            [
                jnp.concatenate(
                    [
                        frames_ref[k, pl.ds(2 * pair + i, span, stride=PITCH), :].astype(BF16)
                        for k in range(2 * POINTS // 128)
                    ],
                    axis=1,
                )
                for i in range(2)
            ],
            axis=0,
        )
        product = lax.dot_general(
            analysis_ref[...], frame, (((1,), (1,)), ((), ())), preferred_element_type=F32
        )
        for i in range(2):
            gain = flags_ref[group * ROWS + 2 * pair + i].astype(F32)
            wide_ref[pl.ds(2 * pair + i, co_rows, stride=PITCH), :] = (
                product[:, i * span : (i + 1) * span] * gain
            )
        return carry

    lax.fori_loop(0, ROWS // 2, transform, 0, unroll=4)

    def send(out, place, row):
        out[place] = wide_ref[pl.ds(pl.multiple_of(row * PITCH, 8), ROWS), :].astype(BF16)

    count, gx_count = counts[0], out_refs[0].shape[0]

    chan_dev = count + counts[1]

    def send_rows(d, carry):
        for k in range(2 * count):
            send(out_refs[0], (d, k // 2, k % 2), d * 2 * chan_dev + k)
        return carry

    lax.fori_loop(0, gx_count, send_rows, 0)
    for k, out in enumerate(out_refs[1:]):
        for slot in range(2):
            owner = me_ref[0] ^ k ^ (slot * (gx_count // 2))
            for j in range(2 * counts[1]):
                send(out, (slot, j // 2, j % 2), (owner * chan_dev + count) * 2 + j)


def spectra_of(samples, flags, me, taper, analysis, gx_count, counts, first, steps, span):
    co_rows = analysis.shape[0]
    rows = steps * ROWS
    out_shape = [jax.ShapeDtypeStruct((gx_count, counts[0], 2, rows, span), BF16)]
    out_specs = [pl.BlockSpec((gx_count, counts[0], 2, ROWS, span), lambda g: (0, 0, 0, g, 0))]
    if counts[1]:
        half = gx_count // 2
        shape = (2, counts[1], 2, rows, span)
        out_shape += [jax.ShapeDtypeStruct(shape, BF16)] * half
        out_specs += [pl.BlockSpec((2, counts[1], 2, ROWS, span), lambda g: (0, 0, 0, g, 0))] * half
    width = samples.shape[2] if steps > 1 or first else (span + TAPS - 1) * POINTS
    return pl.pallas_call(
        functools.partial(spectra_kernel, first, counts),
        out_shape=out_shape,
        grid=(steps,),
        in_specs=[
            pl.BlockSpec(memory_space=pltpu.SMEM),
            pl.BlockSpec(memory_space=pltpu.SMEM),
            pl.BlockSpec((2, ROWS, width), lambda g: (0, (g + first) // 2, 0)),
            pl.BlockSpec((TAPS, POINTS), lambda g: (0, 0)),
            pl.BlockSpec((co_rows, 2 * POINTS), lambda g: (0, 0)),
        ],
        out_specs=out_specs,
        scratch_shapes=[
            pltpu.VMEM((2 * POINTS // 128, span * PITCH, 128), F32),
            pltpu.VMEM((co_rows * PITCH, span), F32),
        ],
        compiler_params=pltpu.CompilerParams(vmem_limit_bytes=VMEM),
        cost_estimate=pl.CostEstimate(
            flops=steps * ROWS * span * co_rows * 4 * POINTS * 3,
            bytes_accessed=steps * ROWS * (samples.shape[2] * 4 + co_rows * span * 2),
            transcendentals=0,
        ),
        name="spectra",
    )(me, flags, samples, taper, analysis)


def weights_kernel(kept_ref, delays_ref, out_ref):
    scale = kept_ref[pl.program_id(0)].astype(F32) * (1.0 / POINTS)
    input_scale = 1.0 / math.sqrt(delays_ref.shape[1])

    def rows(step, carry):
        at = pl.ds(pl.multiple_of(step * 16, 16), 16)
        turns = delays_ref[at, :] * scale
        turns = turns - jnp.floor(turns + 0.5)
        size = jnp.abs(turns)
        near = jnp.minimum(size, 0.5 - size)
        square = near * near
        sine = square * SINE_FIT[-1] + SINE_FIT[-2]
        for value in SINE_FIT[-3::-1]:
            sine = sine * square + value
        sine = sine * (near * input_scale)
        cosine = square * COSINE_FIT[-1] + COSINE_FIT[-2]
        for value in COSINE_FIT[-3::-1]:
            cosine = cosine * square + value
        cosine = cosine * input_scale
        out_ref[0, 0, at, :] = jnp.where(size > 0.25, -cosine, cosine).astype(BF16)
        out_ref[0, 1, at, :] = jnp.where(turns > 0.0, -sine, sine).astype(BF16)
        return carry

    lax.fori_loop(0, delays_ref.shape[0] // 16, rows, 0)


def weights_of(kept, delays):
    beams, inputs = delays.shape
    return pl.pallas_call(
        weights_kernel,
        out_shape=jax.ShapeDtypeStruct((kept.shape[0], 2, beams, inputs), BF16),
        grid=(kept.shape[0],),
        in_specs=[
            pl.BlockSpec(memory_space=pltpu.SMEM),
            pl.BlockSpec((beams, inputs), lambda c: (0, 0)),
        ],
        out_specs=pl.BlockSpec((1, 2, beams, inputs), lambda c: (c, 0, 0, 0)),
        compiler_params=pltpu.CompilerParams(vmem_limit_bytes=VMEM),
        cost_estimate=pl.CostEstimate(
            flops=kept.shape[0] * beams * inputs * 40,
            bytes_accessed=kept.shape[0] * beams * inputs * 4,
            transcendentals=0,
        ),
        name="weights",
    )(kept, delays)


def assemble(me_ref, lead, rest, c, joined_ref):
    sources, _, _, lead_rows, span = lead.shape
    ahead = lead_rows // ROWS
    steps = rest[-1].shape[-2] // ROWS + ahead
    share = steps // 2 * ROWS
    half = sources // 2

    def place(src, o, step, block):
        row = src * share + step // 2 * ROWS
        if not isinstance(row, int):
            row = pl.multiple_of(row, ROWS)
        joined_ref[o, pl.ds(row, ROWS), pl.ds(step % 2 * span, span)] = block

    for k in range(sources):
        for o in range(2):
            for step in range(ahead):
                place(k, o, step, lead[k, c, o, pl.ds(step * ROWS, ROWS), :])
            for step in range(ahead, steps):
                rows = pl.ds((step - ahead) * ROWS, ROWS)
                if len(rest) == 1:
                    place(k, o, step, rest[0][k, c, o, rows, :])
                elif k < half:
                    place(me_ref[0] ^ k, o, step, rest[k][0, c, o, rows, :])
                else:
                    place(me_ref[0] ^ k, o, step, rest[half][k - half, c, o, rows, :])


def beams_kernel(part_count, me_ref, lead, *refs):
    rest, (weights_ref, turn_ref) = refs[:part_count], refs[part_count : part_count + 2]
    each, _, beams, inputs = weights_ref.shape
    out_ref, joined_refs = refs[-1 - each], refs[-each:]
    for c in range(each):
        assemble(me_ref, lead, rest, c, joined_refs[c])
        weights = weights_ref[c].reshape(2 * beams, inputs)
        products = [jnp.dot(weights, joined_refs[c][o], preferred_element_type=F32) for o in range(2)]
        real_part = (products[0][:beams] - products[1][beams:]).astype(BF16).astype(F32)
        imag_part = (products[1][:beams] + products[0][beams:]).astype(BF16).astype(F32)
        cosine, sine = turn_ref[c, :, 0:1], turn_ref[c, :, 1:2]
        turned = [
            (real_part * cosine + imag_part * sine).astype(BF16),
            (imag_part * cosine - real_part * sine).astype(BF16),
        ]
        for x in range(2):
            if len(out_ref.shape) == 5:
                shape = (out_ref.shape[0],) + out_ref.shape[3:]
                out_ref[:, c, x] = turned[x].reshape(shape)
            else:
                out_ref[c, x] = turned[x]


def part_specs(lead, rest, first, at, each):
    specs = [
        pl.BlockSpec(memory_space=pltpu.SMEM),
        pl.BlockSpec((lead.shape[0], each) + lead.shape[2:], lambda c: (0, c + first // each, 0, 0, 0)),
    ]
    for a in rest[:-1]:
        specs.append(pl.BlockSpec((1, each) + a.shape[2:], lambda c: (0, c + at // each, 0, 0, 0)))
    far = rest[-1]
    specs.append(pl.BlockSpec((far.shape[0], each) + far.shape[2:], lambda c: (0, c, 0, 0, 0)))
    return specs


def beams_of(me, lead, rest, weights, turns, first, at, count, held):
    channels, _, beams, inputs = weights.shape
    gx_count, span = lead.shape[0], lead.shape[4]
    spectra_all = 2 * span
    beam_dev = beams // gx_count
    each = EACH if count % EACH == 0 and first % EACH == 0 and at % EACH == 0 else 1
    start = first // each
    if beam_dev % 16 == 0:
        out_shape = (gx_count, channels, 2, beam_dev, spectra_all)
        out_spec = pl.BlockSpec(
            (gx_count, each, 2, beam_dev, spectra_all), lambda c: (0, c + start, 0, 0, 0)
        )
    else:
        out_shape = (channels, 2, beams, spectra_all)
        out_spec = pl.BlockSpec((each, 2, beams, spectra_all), lambda c: (c + start, 0, 0, 0))
    more = [] if held is None else [held]
    return pl.pallas_call(
        functools.partial(beams_kernel, len(rest)),
        out_shape=jax.ShapeDtypeStruct(out_shape, BF16),
        grid=(count // each,),
        in_specs=part_specs(lead, rest, first, at, each)
        + [
            pl.BlockSpec((each, 2, beams, inputs), lambda c: (c + start, 0, 0, 0)),
            pl.BlockSpec((each, beams, 2), lambda c: (c + start, 0, 0)),
        ]
        + [pl.BlockSpec(memory_space=pl.ANY)] * len(more),
        out_specs=out_spec,
        scratch_shapes=[pltpu.VMEM((2, inputs, spectra_all), BF16)] * each,
        input_output_aliases={4 + len(rest): 0} if more else {},
        compiler_params=pltpu.CompilerParams(vmem_limit_bytes=BEAMS_VMEM),
        cost_estimate=pl.CostEstimate(
            flops=count * beams * inputs * spectra_all * 8,
            bytes_accessed=count * inputs * (spectra_all * 4 + beams * 4),
            transcendentals=0,
        ),
        name="beams",
    )(me, lead, *rest, weights, turns, *more)


def gram_kernel(part_count, me_ref, lead, *refs):
    (out_ref, joined_ref) = refs[-2:]
    rest = refs[:part_count]
    assemble(me_ref, lead, rest, 0, joined_ref)
    inputs, spectra_all = joined_ref.shape[1:]
    side = 256
    scale = 1.0 / spectra_all
    contract = (((1,), (1,)), ((), ()))

    def product(left, right, rows, columns):
        return lax.dot_general(
            joined_ref[left, rows], joined_ref[right, columns], contract, preferred_element_type=F32
        )

    for j in range(inputs // side):
        columns = slice(j * side, (j + 1) * side)
        above = slice(0, (j + 1) * side)
        below = slice(j * side, inputs)
        real_sum = product(0, 0, above, columns) + product(1, 1, above, columns)
        mixed = product(1, 0, below, columns) - product(0, 1, below, columns)
        if j:
            out_ref[0, : j * side, columns] = (real_sum[: j * side] * scale).astype(BF16)
        upper = lax.broadcasted_iota(jnp.int32, (side, side), 0) <= lax.broadcasted_iota(
            jnp.int32, (side, side), 1
        )
        out_ref[0, columns, columns] = (
            jnp.where(upper, real_sum[j * side :], mixed[:side]) * scale
        ).astype(BF16)
        if (j + 1) * side < inputs:
            out_ref[0, (j + 1) * side :, columns] = (mixed[side:] * scale).astype(BF16)


def gram_of(me, lead, rest, first, at, count, held):
    sources, channels, _, _, span = lead.shape
    inputs = sources * (rest[-1].shape[-2] + lead.shape[3]) // 2
    more = [] if held is None else [held]
    return pl.pallas_call(
        functools.partial(gram_kernel, len(rest)),
        out_shape=jax.ShapeDtypeStruct((channels, inputs, inputs), BF16),
        grid=(count,),
        in_specs=part_specs(lead, rest, first, at, 1) + [pl.BlockSpec(memory_space=pl.ANY)] * len(more),
        out_specs=pl.BlockSpec((1, inputs, inputs), lambda c: (c + first, 0, 0)),
        scratch_shapes=[pltpu.VMEM((2, inputs, 2 * span), BF16)],
        input_output_aliases={2 + len(rest): 0} if more else {},
        compiler_params=pltpu.CompilerParams(vmem_limit_bytes=VMEM),
        cost_estimate=pl.CostEstimate(
            flops=count * inputs * inputs * span * 10,
            bytes_accessed=count * inputs * (span * 8 + inputs * 2),
            transcendentals=0,
        ),
        name="gram",
    )(me, lead, *rest, *more)


def series_kernel(share, part_count, *refs):
    parts, (synthesis_ref, out_ref, wide_ref) = refs[:part_count], refs[part_count:]
    beam_dev, spectra_all = parts[0].shape[3:]
    rows = synthesis_ref.shape[0]
    pitch = wide_ref.shape[1] // rows
    halves = [slice(k * 128, (k + 1) * 128) for k in range(spectra_all // 128)]

    @pl.when(pl.program_id(0) == 0)
    def _():
        base = 0
        for part in parts:
            each = 2 * part.shape[1]

            def widen_source(d, carry, base=base, part=part, each=each):
                for j in range(each):
                    block = part[d, j // 2, j % 2]
                    row = pl.multiple_of((base + d * each + j) * pitch, 8)
                    for k, half in enumerate(halves):
                        wide_ref[k, pl.ds(row, beam_dev), :] = block[:, half].astype(F32)
                return carry

            lax.fori_loop(0, part.shape[0], widen_source, 0)
            base += part.shape[0] * each

    for b in range(share):
        beam = pl.program_id(0) * share + b
        turned = jnp.concatenate(
            [
                wide_ref[k, pl.ds(beam, rows, stride=pitch), :].astype(BF16)
                for k in range(len(halves))
            ],
            axis=1,
        )
        product = lax.dot_general(
            turned, synthesis_ref[...], (((0,), (0,)), ((), ())), preferred_element_type=F32
        )
        for o in range(2):
            out_ref[o, b] = product[:, o * POINTS : (o + 1) * POINTS]


def series_of(parts, synthesis):
    beam_dev, spectra_all = parts[0].shape[3:]
    rows = synthesis.shape[0]
    pitch = (beam_dev + 7) // 8 // 2 * 16 + 8
    share = SHARE
    return pl.pallas_call(
        functools.partial(series_kernel, share, len(parts)),
        out_shape=jax.ShapeDtypeStruct((2, beam_dev, spectra_all, POINTS), F32),
        grid=(beam_dev // share,),
        in_specs=[pl.BlockSpec(a.shape, lambda b: (0, 0, 0, 0, 0)) for a in parts]
        + [pl.BlockSpec(synthesis.shape, lambda b: (0, 0))],
        out_specs=pl.BlockSpec((2, share, spectra_all, POINTS), lambda b: (0, b, 0, 0)),
        scratch_shapes=[pltpu.VMEM((spectra_all // 128, rows * pitch, 128), F32)],
        compiler_params=pltpu.CompilerParams(vmem_limit_bytes=VMEM),
        cost_estimate=pl.CostEstimate(
            flops=2 * beam_dev * rows * spectra_all * 2 * POINTS,
            bytes_accessed=beam_dev * spectra_all * (rows * 2 + POINTS * 8),
            transcendentals=0,
        ),
        name="series",
    )(*parts, synthesis)


def exchange(array):
    return lax.all_to_all(array, "gx", split_axis=0, concat_axis=0, tiled=True)


tie = lax.optimization_barrier


def swap(array, k, count):
    return lax.ppermute(array, "gx", [(i, i ^ k) for i in range(count)])


def shards(samples, flags, kept_channels, beam_order, dm_bins, delays):
    gx_count = lax.axis_size("gx")
    me = lax.axis_index("gx").astype(jnp.int32)
    channels = kept_channels.shape[0]
    chan_dev = channels // gx_count
    span = (samples.shape[2] // POINTS - TAPS + 1) // 2
    steps = samples.shape[1] // ROWS * 2
    ahead = min(LEAD, steps // 2)
    apart = chan_dev // APART if gx_count <= 16 and gx_count & (gx_count - 1) == 0 else 0
    main = chan_dev - apart
    spot = me.reshape(1)

    taper = jnp.asarray(prototype_taper(TAPS, POINTS))
    cosine, sine = dft_tables(kept_channels, POINTS)
    table = jnp.stack(
        [jnp.concatenate([cosine, sine], 1), jnp.concatenate([-sine, cosine], 1)], 1
    ).astype(BF16)
    table_rows = table.reshape(-1, 2 * POINTS)
    (lead,) = spectra_of(
        samples, flags, spot, taper, table_rows, gx_count, (chan_dev, 0), 0, ahead, span
    )
    spot, lead = tie((spot, lead))
    rest, *near = spectra_of(
        samples, flags, spot, taper, table_rows, gx_count, (main, apart), ahead, steps - ahead, span
    )
    lead = exchange(lead)
    my_kept = lax.dynamic_slice_in_dim(kept_channels, me * chan_dev, chan_dev)
    my_kept, rest = tie((my_kept, rest))
    weights = weights_of(my_kept, jnp.take(delays, beam_order, axis=0))
    turns = jnp.stack(rotation(jnp.take(dm_bins, beam_order), my_kept), 2)

    half = gx_count // 2
    cuts = [(0, apart - 1), (apart - 1, apart)] if apart > 1 else [(0, apart)] * (apart > 0)
    relays = []
    if apart:
        near = near[:1] + [swap(near[k], k, gx_count) for k in range(1, half)]
        relays = [jnp.stack([n[1, a:b] for n in near], 0) for a, b in cuts]
    rest, lead = tie((rest, lead))
    rest = exchange(rest)

    beams, visibilities = None, None
    for order, (a, b) in enumerate(cuts):
        if order == len(cuts) - 1:
            if order:
                rest, relays, beams, visibilities = tie((rest, relays, beams, visibilities))
            else:
                rest, relays = tie((rest, relays))
            far = swap(relays[order], half, gx_count)
            beams = beams_of(spot, lead, [rest], weights, turns, 0, 0, main, beams)
        else:
            far = swap(relays[order], half, gx_count)
        parts = near + [far]
        beams = beams_of(spot, lead, parts, weights, turns, main + a, a, b - a, beams)
        if order < len(cuts) - 1:
            visibilities = gram_of(spot, lead, parts, main + a, a, b - a, visibilities)
    if not cuts:
        beams = beams_of(spot, lead, [rest], weights, turns, 0, 0, main, beams)
    spot, beams = tie((spot, beams))
    if beams.ndim == 4:
        beams = beams.reshape(chan_dev, 2, gx_count, -1, beams.shape[3]).transpose(2, 0, 1, 3, 4)
    sums = exchange(beams)
    visibilities = gram_of(spot, lead, [rest], 0, 0, main, visibilities)
    for a, b in cuts[-1:]:
        visibilities = gram_of(spot, lead, parts, main + a, a, b - a, visibilities)
    series = series_of([sums], table_rows)
    return (visibilities, series)


def solution(mesh):
    placed = (P(None, ("groups", "gx"), None), P("gx"), P(), P(), P("groups"), P("groups", None))
    return jax.shard_map(
        shards,
        mesh=mesh,
        in_specs=placed,
        out_specs=(P(("groups", "gx"), None, None), P(None, ("groups", "gx"), None, None)),
        check_vma=False,
    )
```

```python
import functools
import math

import jax
import jax.numpy as jnp
import numpy as np
from jax import lax
from jax.experimental import pallas as pl
from jax.experimental.pallas import tpu as pltpu
from jax.sharding import PartitionSpec as P

POINTS = 256
TAPS = 8
ROWS = 16
EACH = 3
SHARE = 8
APART = 12
LEAD = 1
PITCH = 24
STRETCH = 16
F32 = jnp.float32
BF16 = jnp.bfloat16
VMEM = 60 * 1024 * 1024
BEAMS_VMEM = VMEM


def fit_tables():
    spots = np.cos(np.pi * (np.arange(4000) + 0.5) / 4000) * 0.125 + 0.125
    powers = np.stack([spots ** (2 * k) for k in range(6)], 1)
    sine = np.linalg.lstsq(powers[:, :5] * spots[:, None], np.sin(2 * np.pi * spots), rcond=None)[0]
    cosine = np.linalg.lstsq(powers, np.cos(2 * np.pi * spots), rcond=None)[0]
    return [float(v) for v in sine], [float(v) for v in cosine]


SINE_FIT, COSINE_FIT = fit_tables()


def prototype_taper(tap_count, point_count):
    spots = np.arange(tap_count * point_count, dtype=np.float64)
    length = float(tap_count * point_count)
    shaped = np.sinc((spots - length / 2.0 + 0.5) / point_count) * (
        0.5 - 0.5 * np.cos(2.0 * math.pi * (spots + 0.5) / length)
    )
    return shaped.reshape(tap_count, point_count).astype(np.float32)


def form_table(kept_ref, table_ref):
    shape = (16, table_ref.shape[1])
    row = lax.broadcasted_iota(jnp.int32, shape, 0)
    column = lax.broadcasted_iota(jnp.int32, shape, 1)
    spot = column & (POINTS - 1)
    quarter = ((row & 1) - jnp.where(column >= POINTS, 1, 0)) * (POINTS // 4)

    def some_rows(block, carry):
        bins = jnp.zeros(shape, jnp.int32)
        for k in range(8):
            bins = jnp.where((row >= 2 * k) & (row < 2 * k + 2), kept_ref[block * 8 + k], bins)
        step = (bins * spot + quarter) & (POINTS - 1)
        step = jnp.minimum(step, POINTS - step)
        near = jnp.minimum(step, POINTS // 2 - step).astype(F32) * (1.0 / POINTS)
        square = near * near
        value = square * COSINE_FIT[-1] + COSINE_FIT[-2]
        for factor in COSINE_FIT[-3::-1]:
            value = value * square + factor
        value = jnp.where(step > POINTS // 4, -value, value) * (1.0 / math.sqrt(POINTS))
        table_ref[pl.ds(pl.multiple_of(block * 16, 16), 16), :] = value.astype(BF16)
        return carry

    lax.fori_loop(0, table_ref.shape[0] // 16, some_rows, 0)


def rotation(dm_rows, kept):
    squares = kept * kept % 4096
    turns = squares[:, None] * dm_rows[None, :] % 4096
    angle = turns.astype(F32) * (2.0 * math.pi / 4096.0)
    return (jnp.cos(angle), jnp.sin(angle))


def spectra_kernel(first, counts, *refs):
    me_ref, flags_ref, samples_ref, taper_ref = refs[:4]
    (frames_ref, wide_ref) = refs[-2:]
    if first:
        analysis_ref, out_refs = refs[4], refs[5:-2]
    else:
        kept_ref, analysis_ref, out_refs = refs[4], refs[5], refs[6:-2]

        @pl.when(pl.program_id(0) == 0)
        def _():
            form_table(kept_ref, analysis_ref)

    span = frames_ref.shape[1] // PITCH
    co_rows = analysis_ref.shape[0]
    step = pl.program_id(0) + first
    group, begin = step // 2, (step % 2) * span

    def form_frames(stretch, carry):
        at = stretch * STRETCH
        for x in range(2):
            for half in range(POINTS // 128):
                lanes = pl.ds(half * 128, 128)
                tapers = [
                    jnp.broadcast_to(taper_ref[pl.ds(t, 1), lanes], (ROWS, 128)) for t in range(TAPS)
                ]
                tiles = []
                for k in range(STRETCH + TAPS - 1):
                    spot = pl.multiple_of((begin + at + k) * POINTS + half * 128, 128)
                    tiles.append(samples_ref[x, :, pl.ds(spot, 128)].astype(F32))
                for s in range(STRETCH):
                    total = tiles[s] * tapers[0]
                    for t in range(1, TAPS):
                        total = total + tiles[s + t] * tapers[t]
                    row = pl.multiple_of((at + s) * PITCH, 8)
                    frames_ref[x * (POINTS // 128) + half, pl.ds(row, ROWS), :] = total
        return carry

    lax.fori_loop(0, span // STRETCH, form_frames, 0)

    def transform(pair, carry):
        frame = jnp.concatenate(
            [
                jnp.concatenate(
                    [
                        frames_ref[k, pl.ds(2 * pair + i, span, stride=PITCH), :].astype(BF16)
                        for k in range(2 * POINTS // 128)
                    ],
                    axis=1,
                )
                for i in range(2)
            ],
            axis=0,
        )
        product = lax.dot_general(
            analysis_ref[...], frame, (((1,), (1,)), ((), ())), preferred_element_type=F32
        )
        for i in range(2):
            gain = flags_ref[group * ROWS + 2 * pair + i].astype(F32)
            wide_ref[pl.ds(2 * pair + i, co_rows, stride=PITCH), :] = (
                product[:, i * span : (i + 1) * span] * gain
            )
        return carry

    lax.fori_loop(0, ROWS // 2, transform, 0, unroll=4)

    def send(out, place, row):
        out[place] = wide_ref[pl.ds(pl.multiple_of(row * PITCH, 8), ROWS), :].astype(BF16)

    count, gx_count = counts[0], out_refs[0].shape[0]

    chan_dev = count + counts[1]

    def send_rows(d, carry):
        for k in range(2 * count):
            send(out_refs[0], (d, k // 2, k % 2), d * 2 * chan_dev + k)
        return carry

    lax.fori_loop(0, gx_count, send_rows, 0)
    for k, out in enumerate(out_refs[1:]):
        for slot in range(2):
            owner = me_ref[0] ^ k ^ (slot * (gx_count // 2))
            for j in range(2 * counts[1]):
                send(out, (slot, j // 2, j % 2), (owner * chan_dev + count) * 2 + j)


def spectra_of(samples, flags, me, taper, given, gx_count, counts, first, steps, span):
    co_rows = given.shape[0] if first else 2 * given.shape[0]
    rows = steps * ROWS
    out_shape = [jax.ShapeDtypeStruct((gx_count, counts[0], 2, rows, span), BF16)]
    out_specs = [pl.BlockSpec((gx_count, counts[0], 2, ROWS, span), lambda g: (0, 0, 0, g, 0))]
    if counts[1]:
        half = gx_count // 2
        shape = (2, counts[1], 2, rows, span)
        out_shape += [jax.ShapeDtypeStruct(shape, BF16)] * half
        out_specs += [pl.BlockSpec((2, counts[1], 2, ROWS, span), lambda g: (0, 0, 0, g, 0))] * half
    table_spec = pl.BlockSpec((co_rows, 2 * POINTS), lambda g: (0, 0))
    if not first:
        out_shape = [jax.ShapeDtypeStruct((co_rows, 2 * POINTS), BF16)] + out_shape
        out_specs = [table_spec] + out_specs
    width = samples.shape[2] if steps > 1 or first else (span + TAPS - 1) * POINTS
    return pl.pallas_call(
        functools.partial(spectra_kernel, first, counts),
        out_shape=out_shape,
        grid=(steps,),
        in_specs=[
            pl.BlockSpec(memory_space=pltpu.SMEM),
            pl.BlockSpec(memory_space=pltpu.SMEM),
            pl.BlockSpec((2, ROWS, width), lambda g: (0, (g + first) // 2, 0)),
            pl.BlockSpec((TAPS, POINTS), lambda g: (0, 0)),
            table_spec if first else pl.BlockSpec(memory_space=pltpu.SMEM),
        ],
        out_specs=out_specs,
        scratch_shapes=[
            pltpu.VMEM((2 * POINTS // 128, span * PITCH, 128), F32),
            pltpu.VMEM((co_rows * PITCH, span), F32),
        ],
        compiler_params=pltpu.CompilerParams(vmem_limit_bytes=VMEM),
        cost_estimate=pl.CostEstimate(
            flops=steps * ROWS * span * co_rows * 4 * POINTS * 3,
            bytes_accessed=steps * ROWS * (samples.shape[2] * 4 + co_rows * span * 2),
            transcendentals=0,
        ),
        name="spectra",
    )(me, flags, samples, taper, given)


def weights_kernel(kept_ref, delays_ref, out_ref):
    scale = kept_ref[pl.program_id(0)].astype(F32) * (1.0 / POINTS)
    input_scale = 1.0 / math.sqrt(delays_ref.shape[1])

    def rows(step, carry):
        at = pl.ds(pl.multiple_of(step * 16, 16), 16)
        turns = delays_ref[at, :] * scale
        turns = turns - jnp.floor(turns + 0.5)
        size = jnp.abs(turns)
        near = jnp.minimum(size, 0.5 - size)
        square = near * near
        sine = square * SINE_FIT[-1] + SINE_FIT[-2]
        for value in SINE_FIT[-3::-1]:
            sine = sine * square + value
        sine = sine * (near * input_scale)
        cosine = square * COSINE_FIT[-1] + COSINE_FIT[-2]
        for value in COSINE_FIT[-3::-1]:
            cosine = cosine * square + value
        cosine = cosine * input_scale
        out_ref[0, 0, at, :] = jnp.where(size > 0.25, -cosine, cosine).astype(BF16)
        out_ref[0, 1, at, :] = jnp.where(turns > 0.0, -sine, sine).astype(BF16)
        return carry

    lax.fori_loop(0, delays_ref.shape[0] // 16, rows, 0)


def weights_of(kept, delays):
    beams, inputs = delays.shape
    return pl.pallas_call(
        weights_kernel,
        out_shape=jax.ShapeDtypeStruct((kept.shape[0], 2, beams, inputs), BF16),
        grid=(kept.shape[0],),
        in_specs=[
            pl.BlockSpec(memory_space=pltpu.SMEM),
            pl.BlockSpec((beams, inputs), lambda c: (0, 0)),
        ],
        out_specs=pl.BlockSpec((1, 2, beams, inputs), lambda c: (c, 0, 0, 0)),
        compiler_params=pltpu.CompilerParams(vmem_limit_bytes=VMEM),
        cost_estimate=pl.CostEstimate(
            flops=kept.shape[0] * beams * inputs * 40,
            bytes_accessed=kept.shape[0] * beams * inputs * 4,
            transcendentals=0,
        ),
        name="weights",
    )(kept, delays)


def assemble(me_ref, lead, rest, c, joined_ref):
    sources, _, _, lead_rows, span = lead.shape
    ahead = lead_rows // ROWS
    steps = rest[-1].shape[-2] // ROWS + ahead
    share = steps // 2 * ROWS
    half = sources // 2

    def place(src, o, step, block):
        row = src * share + step // 2 * ROWS
        if not isinstance(row, int):
            row = pl.multiple_of(row, ROWS)
        joined_ref[o, pl.ds(row, ROWS), pl.ds(step % 2 * span, span)] = block

    for k in range(sources):
        for o in range(2):
            for step in range(ahead):
                place(k, o, step, lead[k, c, o, pl.ds(step * ROWS, ROWS), :])
            for step in range(ahead, steps):
                rows = pl.ds((step - ahead) * ROWS, ROWS)
                if len(rest) == 1:
                    place(k, o, step, rest[0][k, c, o, rows, :])
                elif k < half:
                    place(me_ref[0] ^ k, o, step, rest[k][0, c, o, rows, :])
                else:
                    place(me_ref[0] ^ k, o, step, rest[half][k - half, c, o, rows, :])


def beams_kernel(part_count, me_ref, lead, *refs):
    rest, (weights_ref, turn_ref) = refs[:part_count], refs[part_count : part_count + 2]
    each, _, beams, inputs = weights_ref.shape
    out_ref, joined_refs = refs[-1 - each], refs[-each:]
    for c in range(each):
        assemble(me_ref, lead, rest, c, joined_refs[c])
        weights = weights_ref[c].reshape(2 * beams, inputs)
        products = [jnp.dot(weights, joined_refs[c][o], preferred_element_type=F32) for o in range(2)]
        real_part = (products[0][:beams] - products[1][beams:]).astype(BF16).astype(F32)
        imag_part = (products[1][:beams] + products[0][beams:]).astype(BF16).astype(F32)
        cosine, sine = turn_ref[c, :, 0:1], turn_ref[c, :, 1:2]
        turned = [
            (real_part * cosine + imag_part * sine).astype(BF16),
            (imag_part * cosine - real_part * sine).astype(BF16),
        ]
        for x in range(2):
            if len(out_ref.shape) == 5:
                shape = (out_ref.shape[0],) + out_ref.shape[3:]
                out_ref[:, c, x] = turned[x].reshape(shape)
            else:
                out_ref[c, x] = turned[x]


def part_specs(lead, rest, first, at, each):
    specs = [
        pl.BlockSpec(memory_space=pltpu.SMEM),
        pl.BlockSpec((lead.shape[0], each) + lead.shape[2:], lambda c: (0, c + first // each, 0, 0, 0)),
    ]
    for a in rest[:-1]:
        specs.append(pl.BlockSpec((1, each) + a.shape[2:], lambda c: (0, c + at // each, 0, 0, 0)))
    far = rest[-1]
    specs.append(pl.BlockSpec((far.shape[0], each) + far.shape[2:], lambda c: (0, c, 0, 0, 0)))
    return specs


def beams_of(me, lead, rest, weights, turns, first, at, count, held):
    channels, _, beams, inputs = weights.shape
    gx_count, span = lead.shape[0], lead.shape[4]
    spectra_all = 2 * span
    beam_dev = beams // gx_count
    each = EACH if count % EACH == 0 and first % EACH == 0 and at % EACH == 0 else 1
    start = first // each
    if beam_dev % 16 == 0:
        out_shape = (gx_count, channels, 2, beam_dev, spectra_all)
        out_spec = pl.BlockSpec(
            (gx_count, each, 2, beam_dev, spectra_all), lambda c: (0, c + start, 0, 0, 0)
        )
    else:
        out_shape = (channels, 2, beams, spectra_all)
        out_spec = pl.BlockSpec((each, 2, beams, spectra_all), lambda c: (c + start, 0, 0, 0))
    more = [] if held is None else [held]
    return pl.pallas_call(
        functools.partial(beams_kernel, len(rest)),
        out_shape=jax.ShapeDtypeStruct(out_shape, BF16),
        grid=(count // each,),
        in_specs=part_specs(lead, rest, first, at, each)
        + [
            pl.BlockSpec((each, 2, beams, inputs), lambda c: (c + start, 0, 0, 0)),
            pl.BlockSpec((each, beams, 2), lambda c: (c + start, 0, 0)),
        ]
        + [pl.BlockSpec(memory_space=pl.ANY)] * len(more),
        out_specs=out_spec,
        scratch_shapes=[pltpu.VMEM((2, inputs, spectra_all), BF16)] * each,
        input_output_aliases={4 + len(rest): 0} if more else {},
        compiler_params=pltpu.CompilerParams(vmem_limit_bytes=BEAMS_VMEM),
        cost_estimate=pl.CostEstimate(
            flops=count * beams * inputs * spectra_all * 8,
            bytes_accessed=count * inputs * (spectra_all * 4 + beams * 4),
            transcendentals=0,
        ),
        name="beams",
    )(me, lead, *rest, weights, turns, *more)


def gram_kernel(part_count, me_ref, lead, *refs):
    (out_ref, joined_ref) = refs[-2:]
    rest = refs[:part_count]
    assemble(me_ref, lead, rest, 0, joined_ref)
    inputs, spectra_all = joined_ref.shape[1:]
    side = 256
    scale = 1.0 / spectra_all
    contract = (((1,), (1,)), ((), ()))

    def product(left, right, rows, columns):
        return lax.dot_general(
            joined_ref[left, rows], joined_ref[right, columns], contract, preferred_element_type=F32
        )

    for j in range(inputs // side):
        columns = slice(j * side, (j + 1) * side)
        above = slice(0, (j + 1) * side)
        below = slice(j * side, inputs)
        real_sum = product(0, 0, above, columns) + product(1, 1, above, columns)
        mixed = product(1, 0, below, columns) - product(0, 1, below, columns)
        if j:
            out_ref[0, : j * side, columns] = (real_sum[: j * side] * scale).astype(BF16)
        upper = lax.broadcasted_iota(jnp.int32, (side, side), 0) <= lax.broadcasted_iota(
            jnp.int32, (side, side), 1
        )
        out_ref[0, columns, columns] = (
            jnp.where(upper, real_sum[j * side :], mixed[:side]) * scale
        ).astype(BF16)
        if (j + 1) * side < inputs:
            out_ref[0, (j + 1) * side :, columns] = (mixed[side:] * scale).astype(BF16)


def gram_of(me, lead, rest, first, at, count, held):
    sources, channels, _, _, span = lead.shape
    inputs = sources * (rest[-1].shape[-2] + lead.shape[3]) // 2
    more = [] if held is None else [held]
    return pl.pallas_call(
        functools.partial(gram_kernel, len(rest)),
        out_shape=jax.ShapeDtypeStruct((channels, inputs, inputs), BF16),
        grid=(count,),
        in_specs=part_specs(lead, rest, first, at, 1) + [pl.BlockSpec(memory_space=pl.ANY)] * len(more),
        out_specs=pl.BlockSpec((1, inputs, inputs), lambda c: (c + first, 0, 0)),
        scratch_shapes=[pltpu.VMEM((2, inputs, 2 * span), BF16)],
        input_output_aliases={2 + len(rest): 0} if more else {},
        compiler_params=pltpu.CompilerParams(vmem_limit_bytes=VMEM),
        cost_estimate=pl.CostEstimate(
            flops=count * inputs * inputs * span * 10,
            bytes_accessed=count * inputs * (span * 8 + inputs * 2),
            transcendentals=0,
        ),
        name="gram",
    )(me, lead, *rest, *more)


def series_kernel(share, part_count, *refs):
    parts, (synthesis_ref, out_ref, wide_ref) = refs[:part_count], refs[part_count:]
    beam_dev, spectra_all = parts[0].shape[3:]
    rows = synthesis_ref.shape[0]
    pitch = wide_ref.shape[1] // rows
    halves = [slice(k * 128, (k + 1) * 128) for k in range(spectra_all // 128)]

    @pl.when(pl.program_id(0) == 0)
    def _():
        base = 0
        for part in parts:
            each = 2 * part.shape[1]

            def widen_source(d, carry, base=base, part=part, each=each):
                for j in range(each):
                    block = part[d, j // 2, j % 2]
                    row = pl.multiple_of((base + d * each + j) * pitch, 8)
                    for k, half in enumerate(halves):
                        wide_ref[k, pl.ds(row, beam_dev), :] = block[:, half].astype(F32)
                return carry

            lax.fori_loop(0, part.shape[0], widen_source, 0)
            base += part.shape[0] * each

    for b in range(share):
        beam = pl.program_id(0) * share + b
        turned = jnp.concatenate(
            [
                wide_ref[k, pl.ds(beam, rows, stride=pitch), :].astype(BF16)
                for k in range(len(halves))
            ],
            axis=1,
        )
        product = lax.dot_general(
            turned, synthesis_ref[...], (((0,), (0,)), ((), ())), preferred_element_type=F32
        )
        for o in range(2):
            out_ref[o, b] = product[:, o * POINTS : (o + 1) * POINTS]


def series_of(parts, synthesis):
    beam_dev, spectra_all = parts[0].shape[3:]
    rows = synthesis.shape[0]
    pitch = (beam_dev + 7) // 8 // 2 * 16 + 8
    share = SHARE
    return pl.pallas_call(
        functools.partial(series_kernel, share, len(parts)),
        out_shape=jax.ShapeDtypeStruct((2, beam_dev, spectra_all, POINTS), F32),
        grid=(beam_dev // share,),
        in_specs=[pl.BlockSpec(a.shape, lambda b: (0, 0, 0, 0, 0)) for a in parts]
        + [pl.BlockSpec(synthesis.shape, lambda b: (0, 0))],
        out_specs=pl.BlockSpec((2, share, spectra_all, POINTS), lambda b: (0, b, 0, 0)),
        scratch_shapes=[pltpu.VMEM((spectra_all // 128, rows * pitch, 128), F32)],
        compiler_params=pltpu.CompilerParams(vmem_limit_bytes=VMEM),
        cost_estimate=pl.CostEstimate(
            flops=2 * beam_dev * rows * spectra_all * 2 * POINTS,
            bytes_accessed=beam_dev * spectra_all * (rows * 2 + POINTS * 8),
            transcendentals=0,
        ),
        name="series",
    )(*parts, synthesis)


def exchange(array):
    return lax.all_to_all(array, "gx", split_axis=0, concat_axis=0, tiled=True)


tie = lax.optimization_barrier


def swap(array, k, count):
    return lax.ppermute(array, "gx", [(i, i ^ k) for i in range(count)])


def shards(samples, flags, kept_channels, beam_order, dm_bins, delays):
    gx_count = lax.axis_size("gx")
    me = lax.axis_index("gx").astype(jnp.int32)
    channels = kept_channels.shape[0]
    chan_dev = channels // gx_count
    span = (samples.shape[2] // POINTS - TAPS + 1) // 2
    steps = samples.shape[1] // ROWS * 2
    ahead = min(LEAD, steps // 2)
    apart = chan_dev // APART if gx_count <= 16 and gx_count & (gx_count - 1) == 0 else 0
    main = chan_dev - apart
    spot = me.reshape(1)

    taper = jnp.asarray(prototype_taper(TAPS, POINTS))
    table_rows, lead = spectra_of(
        samples, flags, spot, taper, kept_channels, gx_count, (chan_dev, 0), 0, ahead, span
    )
    spot, lead = tie((spot, lead))
    rest, *near = spectra_of(
        samples, flags, spot, taper, table_rows, gx_count, (main, apart), ahead, steps - ahead, span
    )
    lead = exchange(lead)
    my_kept = lax.dynamic_slice_in_dim(kept_channels, me * chan_dev, chan_dev)
    my_kept, rest = tie((my_kept, rest))
    weights = weights_of(my_kept, jnp.take(delays, beam_order, axis=0))
    turns = jnp.stack(rotation(jnp.take(dm_bins, beam_order), my_kept), 2)

    half = gx_count // 2
    cuts = [(0, apart - 1), (apart - 1, apart)] if apart > 1 else [(0, apart)] * (apart > 0)
    relays = []
    if apart:
        near = near[:1] + [swap(near[k], k, gx_count) for k in range(1, half)]
        relays = [jnp.stack([n[1, a:b] for n in near], 0) for a, b in cuts]
    rest, lead = tie((rest, lead))
    rest = exchange(rest)

    beams, visibilities = None, None
    for order, (a, b) in enumerate(cuts):
        if order == len(cuts) - 1:
            if order:
                rest, relays, beams, visibilities = tie((rest, relays, beams, visibilities))
            else:
                rest, relays = tie((rest, relays))
            far = swap(relays[order], half, gx_count)
            beams = beams_of(spot, lead, [rest], weights, turns, 0, 0, main, beams)
        else:
            far = swap(relays[order], half, gx_count)
        parts = near + [far]
        beams = beams_of(spot, lead, parts, weights, turns, main + a, a, b - a, beams)
        if order < len(cuts) - 1:
            visibilities = gram_of(spot, lead, parts, main + a, a, b - a, visibilities)
    if not cuts:
        beams = beams_of(spot, lead, [rest], weights, turns, 0, 0, main, beams)
    spot, beams = tie((spot, beams))
    if beams.ndim == 4:
        beams = beams.reshape(chan_dev, 2, gx_count, -1, beams.shape[3]).transpose(2, 0, 1, 3, 4)
    sums = exchange(beams)
    visibilities = gram_of(spot, lead, [rest], 0, 0, main, visibilities)
    for a, b in cuts[-1:]:
        visibilities = gram_of(spot, lead, parts, main + a, a, b - a, visibilities)
    series = series_of([sums], table_rows)
    return (visibilities, series)


def solution(mesh):
    placed = (P(None, ("groups", "gx"), None), P("gx"), P(), P(), P("groups"), P("groups", None))
    return jax.shard_map(
        shards,
        mesh=mesh,
        in_specs=placed,
        out_specs=(P(("groups", "gx"), None, None), P(None, ("groups", "gx"), None, None)),
        check_vma=False,
    )
```

```python
import functools
import math

import jax
import jax.numpy as jnp
import numpy as np
from jax import lax
from jax.experimental import pallas as pl
from jax.experimental.pallas import tpu as pltpu
from jax.sharding import PartitionSpec as P

POINTS = 256
TAPS = 8
ROWS = 16
EACH = 3
SHARE = 8
APART = 12
LEAD = 1
PITCH = 24
STRETCH = 16
F32 = jnp.float32
BF16 = jnp.bfloat16
VMEM = 60 * 1024 * 1024
BEAMS_VMEM = VMEM


def fit_tables():
    spots = np.cos(np.pi * (np.arange(4000) + 0.5) / 4000) * 0.125 + 0.125
    powers = np.stack([spots ** (2 * k) for k in range(6)], 1)
    sine = np.linalg.lstsq(powers[:, :5] * spots[:, None], np.sin(2 * np.pi * spots), rcond=None)[0]
    cosine = np.linalg.lstsq(powers, np.cos(2 * np.pi * spots), rcond=None)[0]
    return [float(v) for v in sine], [float(v) for v in cosine]


SINE_FIT, COSINE_FIT = fit_tables()


def prototype_taper(tap_count, point_count):
    spots = np.arange(tap_count * point_count, dtype=np.float64)
    length = float(tap_count * point_count)
    shaped = np.sinc((spots - length / 2.0 + 0.5) / point_count) * (
        0.5 - 0.5 * np.cos(2.0 * math.pi * (spots + 0.5) / length)
    )
    return shaped.reshape(tap_count, point_count).astype(np.float32)


def form_table(kept_ref, table_ref):
    shape = (16, table_ref.shape[1])
    row = lax.broadcasted_iota(jnp.int32, shape, 0)
    column = lax.broadcasted_iota(jnp.int32, shape, 1)
    spot = column & (POINTS - 1)
    quarter = ((row & 1) - jnp.where(column >= POINTS, 1, 0)) * (POINTS // 4)

    def some_rows(block, carry):
        bins = jnp.zeros(shape, jnp.int32)
        for k in range(8):
            bins = jnp.where((row >= 2 * k) & (row < 2 * k + 2), kept_ref[block * 8 + k], bins)
        step = (bins * spot + quarter) & (POINTS - 1)
        step = jnp.minimum(step, POINTS - step)
        near = jnp.minimum(step, POINTS // 2 - step).astype(F32) * (1.0 / POINTS)
        square = near * near
        value = square * COSINE_FIT[-1] + COSINE_FIT[-2]
        for factor in COSINE_FIT[-3::-1]:
            value = value * square + factor
        value = jnp.where(step > POINTS // 4, -value, value) * (1.0 / math.sqrt(POINTS))
        table_ref[pl.ds(pl.multiple_of(block * 16, 16), 16), :] = value.astype(BF16)
        return carry

    lax.fori_loop(0, table_ref.shape[0] // 16, some_rows, 0)


def rotation(dm_rows, kept):
    squares = kept * kept % 4096
    turns = squares[:, None] * dm_rows[None, :] % 4096
    angle = turns.astype(F32) * (2.0 * math.pi / 4096.0)
    return (jnp.cos(angle), jnp.sin(angle))


def spectra_kernel(first, counts, *refs):
    me_ref, flags_ref, samples_ref, taper_ref = refs[:4]
    (frames_ref, wide_ref) = refs[-2:]
    if first:
        analysis_ref, out_refs = refs[4], refs[5:-2]
    else:
        kept_ref, analysis_ref, out_refs = refs[4], refs[5], refs[6:-2]

        @pl.when(pl.program_id(0) == 0)
        def _():
            form_table(kept_ref, analysis_ref)

    span = frames_ref.shape[1] // PITCH
    co_rows = analysis_ref.shape[0]
    step = pl.program_id(0) + first
    group, begin = step // 2, (step % 2) * span

    def form_frames(stretch, carry):
        at = stretch * STRETCH
        for x in range(2):
            for half in range(POINTS // 128):
                lanes = pl.ds(half * 128, 128)
                tapers = [
                    jnp.broadcast_to(taper_ref[pl.ds(t, 1), lanes], (ROWS, 128)) for t in range(TAPS)
                ]
                tiles = []
                for k in range(STRETCH + TAPS - 1):
                    spot = pl.multiple_of((begin + at + k) * POINTS + half * 128, 128)
                    tiles.append(samples_ref[x, :, pl.ds(spot, 128)].astype(F32))
                for s in range(STRETCH):
                    total = tiles[s] * tapers[0]
                    for t in range(1, TAPS):
                        total = total + tiles[s + t] * tapers[t]
                    row = pl.multiple_of((at + s) * PITCH, 8)
                    frames_ref[x * (POINTS // 128) + half, pl.ds(row, ROWS), :] = total
        return carry

    lax.fori_loop(0, span // STRETCH, form_frames, 0)

    def transform(pair, carry):
        frame = jnp.concatenate(
            [
                jnp.concatenate(
                    [
                        frames_ref[k, pl.ds(2 * pair + i, span, stride=PITCH), :].astype(BF16)
                        for k in range(2 * POINTS // 128)
                    ],
                    axis=1,
                )
                for i in range(2)
            ],
            axis=0,
        )
        product = lax.dot_general(
            analysis_ref[...], frame, (((1,), (1,)), ((), ())), preferred_element_type=F32
        )
        for i in range(2):
            gain = flags_ref[group * ROWS + 2 * pair + i].astype(F32)
            wide_ref[pl.ds(2 * pair + i, co_rows, stride=PITCH), :] = (
                product[:, i * span : (i + 1) * span] * gain
            )
        return carry

    lax.fori_loop(0, ROWS // 2, transform, 0, unroll=4)

    def send(out, place, row):
        out[place] = wide_ref[pl.ds(pl.multiple_of(row * PITCH, 8), ROWS), :].astype(BF16)

    count, gx_count = counts[0], out_refs[0].shape[0]

    chan_dev = count + counts[1]

    def send_rows(d, carry):
        for k in range(2 * count):
            send(out_refs[0], (d, k // 2, k % 2), d * 2 * chan_dev + k)
        return carry

    lax.fori_loop(0, gx_count, send_rows, 0)
    for k, out in enumerate(out_refs[1:]):
        for slot in range(2):
            owner = me_ref[0] ^ k ^ (slot * (gx_count // 2))
            for j in range(2 * counts[1]):
                send(out, (slot, j // 2, j % 2), (owner * chan_dev + count) * 2 + j)


def spectra_of(samples, flags, me, taper, given, gx_count, counts, first, steps, span):
    co_rows = given.shape[0] if first else 2 * given.shape[0]
    rows = steps * ROWS
    out_shape = [jax.ShapeDtypeStruct((gx_count, counts[0], 2, rows, span), BF16)]
    out_specs = [pl.BlockSpec((gx_count, counts[0], 2, ROWS, span), lambda g: (0, 0, 0, g, 0))]
    if counts[1]:
        half = gx_count // 2
        shape = (2, counts[1], 2, rows, span)
        out_shape += [jax.ShapeDtypeStruct(shape, BF16)] * half
        out_specs += [pl.BlockSpec((2, counts[1], 2, ROWS, span), lambda g: (0, 0, 0, g, 0))] * half
    table_spec = pl.BlockSpec((co_rows, 2 * POINTS), lambda g: (0, 0))
    if not first:
        out_shape = [jax.ShapeDtypeStruct((co_rows, 2 * POINTS), BF16)] + out_shape
        out_specs = [table_spec] + out_specs
    width = samples.shape[2] if steps > 1 or first else (span + TAPS - 1) * POINTS
    return pl.pallas_call(
        functools.partial(spectra_kernel, first, counts),
        out_shape=out_shape,
        grid=(steps,),
        in_specs=[
            pl.BlockSpec(memory_space=pltpu.SMEM),
            pl.BlockSpec(memory_space=pltpu.SMEM),
            pl.BlockSpec((2, ROWS, width), lambda g: (0, (g + first) // 2, 0)),
            pl.BlockSpec((TAPS, POINTS), lambda g: (0, 0)),
            table_spec if first else pl.BlockSpec(memory_space=pltpu.SMEM),
        ],
        out_specs=out_specs,
        scratch_shapes=[
            pltpu.VMEM((2 * POINTS // 128, span * PITCH, 128), F32),
            pltpu.VMEM((co_rows * PITCH, span), F32),
        ],
        compiler_params=pltpu.CompilerParams(vmem_limit_bytes=VMEM),
        cost_estimate=pl.CostEstimate(
            flops=steps * ROWS * span * co_rows * 4 * POINTS * 3,
            bytes_accessed=steps * ROWS * (samples.shape[2] * 4 + co_rows * span * 2),
            transcendentals=0,
        ),
        name="spectra",
    )(me, flags, samples, taper, given)


def weights_kernel(kept_ref, delays_ref, out_ref):
    scale = kept_ref[pl.program_id(0)].astype(F32) * (1.0 / POINTS)
    input_scale = 1.0 / math.sqrt(delays_ref.shape[1])

    def rows(step, carry):
        at = pl.ds(pl.multiple_of(step * 16, 16), 16)
        turns = delays_ref[at, :] * scale
        turns = turns - jnp.floor(turns + 0.5)
        size = jnp.abs(turns)
        near = jnp.minimum(size, 0.5 - size)
        square = near * near
        sine = square * SINE_FIT[-1] + SINE_FIT[-2]
        for value in SINE_FIT[-3::-1]:
            sine = sine * square + value
        sine = sine * (near * input_scale)
        cosine = square * COSINE_FIT[-1] + COSINE_FIT[-2]
        for value in COSINE_FIT[-3::-1]:
            cosine = cosine * square + value
        cosine = cosine * input_scale
        out_ref[0, 0, at, :] = jnp.where(size > 0.25, -cosine, cosine).astype(BF16)
        out_ref[0, 1, at, :] = jnp.where(turns > 0.0, -sine, sine).astype(BF16)
        return carry

    lax.fori_loop(0, delays_ref.shape[0] // 16, rows, 0)


def weights_of(kept, delays):
    beams, inputs = delays.shape
    return pl.pallas_call(
        weights_kernel,
        out_shape=jax.ShapeDtypeStruct((kept.shape[0], 2, beams, inputs), BF16),
        grid=(kept.shape[0],),
        in_specs=[
            pl.BlockSpec(memory_space=pltpu.SMEM),
            pl.BlockSpec((beams, inputs), lambda c: (0, 0)),
        ],
        out_specs=pl.BlockSpec((1, 2, beams, inputs), lambda c: (c, 0, 0, 0)),
        compiler_params=pltpu.CompilerParams(vmem_limit_bytes=VMEM),
        cost_estimate=pl.CostEstimate(
            flops=kept.shape[0] * beams * inputs * 40,
            bytes_accessed=kept.shape[0] * beams * inputs * 4,
            transcendentals=0,
        ),
        name="weights",
    )(kept, delays)


def assemble(me_ref, lead, rest, c, joined_ref):
    sources, _, _, lead_rows, span = lead.shape
    ahead = lead_rows // ROWS
    steps = rest[-1].shape[-2] // ROWS + ahead
    share = steps // 2 * ROWS
    half = sources // 2

    def place(src, o, step, block):
        row = src * share + step // 2 * ROWS
        if not isinstance(row, int):
            row = pl.multiple_of(row, ROWS)
        joined_ref[o, pl.ds(row, ROWS), pl.ds(step % 2 * span, span)] = block

    for k in range(sources):
        for o in range(2):
            for step in range(ahead):
                place(k, o, step, lead[k, c, o, pl.ds(step * ROWS, ROWS), :])
            for step in range(ahead, steps):
                rows = pl.ds((step - ahead) * ROWS, ROWS)
                if len(rest) == 1:
                    place(k, o, step, rest[0][k, c, o, rows, :])
                elif k < half:
                    place(me_ref[0] ^ k, o, step, rest[k][0, c, o, rows, :])
                else:
                    place(me_ref[0] ^ k, o, step, rest[half][k - half, c, o, rows, :])


def beams_kernel(part_count, me_ref, lead, *refs):
    rest, (weights_ref, turn_ref) = refs[:part_count], refs[part_count : part_count + 2]
    each, _, beams, inputs = weights_ref.shape
    out_ref, joined_refs = refs[-1 - each], refs[-each:]
    for c in range(each):
        assemble(me_ref, lead, rest, c, joined_refs[c])
        weights = weights_ref[c].reshape(2 * beams, inputs)
        products = [jnp.dot(weights, joined_refs[c][o], preferred_element_type=F32) for o in range(2)]
        real_part = (products[0][:beams] - products[1][beams:]).astype(BF16).astype(F32)
        imag_part = (products[1][:beams] + products[0][beams:]).astype(BF16).astype(F32)
        cosine, sine = turn_ref[c, :, 0:1], turn_ref[c, :, 1:2]
        turned = [
            (real_part * cosine + imag_part * sine).astype(BF16),
            (imag_part * cosine - real_part * sine).astype(BF16),
        ]
        for x in range(2):
            if len(out_ref.shape) == 5:
                shape = (out_ref.shape[0],) + out_ref.shape[3:]
                out_ref[:, c, x] = turned[x].reshape(shape)
            else:
                out_ref[c, x] = turned[x]


def part_specs(lead, rest, first, at, each):
    specs = [
        pl.BlockSpec(memory_space=pltpu.SMEM),
        pl.BlockSpec((lead.shape[0], each) + lead.shape[2:], lambda c: (0, c + first // each, 0, 0, 0)),
    ]
    for a in rest[:-1]:
        specs.append(pl.BlockSpec((1, each) + a.shape[2:], lambda c: (0, c + at // each, 0, 0, 0)))
    far = rest[-1]
    specs.append(pl.BlockSpec((far.shape[0], each) + far.shape[2:], lambda c: (0, c, 0, 0, 0)))
    return specs


def beams_of(me, lead, rest, weights, turns, first, at, count, held):
    channels, _, beams, inputs = weights.shape
    gx_count, span = lead.shape[0], lead.shape[4]
    spectra_all = 2 * span
    beam_dev = beams // gx_count
    each = EACH if count % EACH == 0 and first % EACH == 0 and at % EACH == 0 else 1
    start = first // each
    if beam_dev % 16 == 0:
        out_shape = (gx_count, channels, 2, beam_dev, spectra_all)
        out_spec = pl.BlockSpec(
            (gx_count, each, 2, beam_dev, spectra_all), lambda c: (0, c + start, 0, 0, 0)
        )
    else:
        out_shape = (channels, 2, beams, spectra_all)
        out_spec = pl.BlockSpec((each, 2, beams, spectra_all), lambda c: (c + start, 0, 0, 0))
    more = [] if held is None else [held]
    return pl.pallas_call(
        functools.partial(beams_kernel, len(rest)),
        out_shape=jax.ShapeDtypeStruct(out_shape, BF16),
        grid=(count // each,),
        in_specs=part_specs(lead, rest, first, at, each)
        + [
            pl.BlockSpec((each, 2, beams, inputs), lambda c: (c + start, 0, 0, 0)),
            pl.BlockSpec((each, beams, 2), lambda c: (c + start, 0, 0)),
        ]
        + [pl.BlockSpec(memory_space=pl.ANY)] * len(more),
        out_specs=out_spec,
        scratch_shapes=[pltpu.VMEM((2, inputs, spectra_all), BF16)] * each,
        input_output_aliases={4 + len(rest): 0} if more else {},
        compiler_params=pltpu.CompilerParams(vmem_limit_bytes=BEAMS_VMEM),
        cost_estimate=pl.CostEstimate(
            flops=count * beams * inputs * spectra_all * 8,
            bytes_accessed=count * inputs * (spectra_all * 4 + beams * 4),
            transcendentals=0,
        ),
        name="beams",
    )(me, lead, *rest, weights, turns, *more)


def gram_kernel(part_count, me_ref, lead, *refs):
    (out_ref, joined_ref) = refs[-2:]
    rest = refs[:part_count]
    assemble(me_ref, lead, rest, 0, joined_ref)
    inputs, spectra_all = joined_ref.shape[1:]
    side = 256
    scale = 1.0 / spectra_all
    contract = (((1,), (1,)), ((), ()))

    def product(left, right, rows, columns):
        return lax.dot_general(
            joined_ref[left, rows], joined_ref[right, columns], contract, preferred_element_type=F32
        )

    for j in range(inputs // side):
        columns = slice(j * side, (j + 1) * side)
        above = slice(0, (j + 1) * side)
        below = slice(j * side, inputs)
        real_sum = product(0, 0, above, columns) + product(1, 1, above, columns)
        mixed = product(1, 0, below, columns) - product(0, 1, below, columns)
        if j:
            out_ref[0, : j * side, columns] = (real_sum[: j * side] * scale).astype(BF16)
        upper = lax.broadcasted_iota(jnp.int32, (side, side), 0) <= lax.broadcasted_iota(
            jnp.int32, (side, side), 1
        )
        out_ref[0, columns, columns] = (
            jnp.where(upper, real_sum[j * side :], mixed[:side]) * scale
        ).astype(BF16)
        if (j + 1) * side < inputs:
            out_ref[0, (j + 1) * side :, columns] = (mixed[side:] * scale).astype(BF16)


def gram_of(me, lead, rest, first, at, count, held):
    sources, channels, _, _, span = lead.shape
    inputs = sources * (rest[-1].shape[-2] + lead.shape[3]) // 2
    more = [] if held is None else [held]
    return pl.pallas_call(
        functools.partial(gram_kernel, len(rest)),
        out_shape=jax.ShapeDtypeStruct((channels, inputs, inputs), BF16),
        grid=(count,),
        in_specs=part_specs(lead, rest, first, at, 1) + [pl.BlockSpec(memory_space=pl.ANY)] * len(more),
        out_specs=pl.BlockSpec((1, inputs, inputs), lambda c: (c + first, 0, 0)),
        scratch_shapes=[pltpu.VMEM((2, inputs, 2 * span), BF16)],
        input_output_aliases={2 + len(rest): 0} if more else {},
        compiler_params=pltpu.CompilerParams(vmem_limit_bytes=VMEM),
        cost_estimate=pl.CostEstimate(
            flops=count * inputs * inputs * span * 10,
            bytes_accessed=count * inputs * (span * 8 + inputs * 2),
            transcendentals=0,
        ),
        name="gram",
    )(me, lead, *rest, *more)


def series_kernel(share, part_count, *refs):
    parts, (synthesis_ref, out_ref, wide_ref) = refs[:part_count], refs[part_count:]
    beam_dev, spectra_all = parts[0].shape[3:]
    rows = synthesis_ref.shape[0]
    pitch = wide_ref.shape[1] // rows
    halves = [slice(k * 128, (k + 1) * 128) for k in range(spectra_all // 128)]

    @pl.when(pl.program_id(0) == 0)
    def _():
        base = 0
        for part in parts:
            each = 2 * part.shape[1]

            def widen_source(d, carry, base=base, part=part, each=each):
                for j in range(each):
                    block = part[d, j // 2, j % 2]
                    row = pl.multiple_of((base + d * each + j) * pitch, 8)
                    for k, half in enumerate(halves):
                        wide_ref[k, pl.ds(row, beam_dev), :] = block[:, half].astype(F32)
                return carry

            lax.fori_loop(0, part.shape[0], widen_source, 0)
            base += part.shape[0] * each

    for b in range(share):
        beam = pl.program_id(0) * share + b
        turned = jnp.concatenate(
            [
                wide_ref[k, pl.ds(beam, rows, stride=pitch), :].astype(BF16)
                for k in range(len(halves))
            ],
            axis=1,
        )
        product = lax.dot_general(
            turned, synthesis_ref[...], (((0,), (0,)), ((), ())), preferred_element_type=F32
        )
        for o in range(2):
            out_ref[o, b] = product[:, o * POINTS : (o + 1) * POINTS]


def series_of(parts, synthesis):
    beam_dev, spectra_all = parts[0].shape[3:]
    rows = synthesis.shape[0]
    pitch = (beam_dev + 7) // 8 // 2 * 16 + 8
    share = SHARE
    return pl.pallas_call(
        functools.partial(series_kernel, share, len(parts)),
        out_shape=jax.ShapeDtypeStruct((2, beam_dev, spectra_all, POINTS), F32),
        grid=(beam_dev // share,),
        in_specs=[pl.BlockSpec(a.shape, lambda b: (0, 0, 0, 0, 0)) for a in parts]
        + [pl.BlockSpec(synthesis.shape, lambda b: (0, 0))],
        out_specs=pl.BlockSpec((2, share, spectra_all, POINTS), lambda b: (0, b, 0, 0)),
        scratch_shapes=[pltpu.VMEM((spectra_all // 128, rows * pitch, 128), F32)],
        compiler_params=pltpu.CompilerParams(vmem_limit_bytes=VMEM),
        cost_estimate=pl.CostEstimate(
            flops=2 * beam_dev * rows * spectra_all * 2 * POINTS,
            bytes_accessed=beam_dev * spectra_all * (rows * 2 + POINTS * 8),
            transcendentals=0,
        ),
        name="series",
    )(*parts, synthesis)


def exchange(array):
    return lax.all_to_all(array, "gx", split_axis=0, concat_axis=0, tiled=True)


tie = lax.optimization_barrier


def swap(array, k, count):
    return lax.ppermute(array, "gx", [(i, i ^ k) for i in range(count)])


def shards(samples, flags, kept_channels, beam_order, dm_bins, delays):
    gx_count = lax.axis_size("gx")
    me = lax.axis_index("gx").astype(jnp.int32)
    channels = kept_channels.shape[0]
    chan_dev = channels // gx_count
    span = (samples.shape[2] // POINTS - TAPS + 1) // 2
    steps = samples.shape[1] // ROWS * 2
    ahead = min(LEAD, steps // 2)
    apart = chan_dev // APART if gx_count <= 16 and gx_count & (gx_count - 1) == 0 else 0
    main = chan_dev - apart
    spot = me.reshape(1)

    taper = jnp.asarray(prototype_taper(TAPS, POINTS))
    table_rows, lead = spectra_of(
        samples, flags, spot, taper, kept_channels, gx_count, (chan_dev, 0), 0, ahead, span
    )
    spot, lead = tie((spot, lead))
    rest, *near = spectra_of(
        samples, flags, spot, taper, table_rows, gx_count, (main, apart), ahead, steps - ahead, span
    )
    lead = exchange(lead)
    my_kept = lax.dynamic_slice_in_dim(kept_channels, me * chan_dev, chan_dev)
    my_kept, rest = tie((my_kept, rest))
    weights = weights_of(my_kept, jnp.take(delays, beam_order, axis=0))
    turns = jnp.stack(rotation(jnp.take(dm_bins, beam_order), my_kept), 2)

    half = gx_count // 2
    cuts = [(0, apart - 1), (apart - 1, apart)] if apart > 1 else [(0, apart)] * (apart > 0)
    relays = []
    if apart:
        near = near[:1] + [swap(near[k], k, gx_count) for k in range(1, half)]
        relays = [jnp.stack([n[1, a:b] for n in near], 0) for a, b in cuts]
    rest, mark = tie((rest, lead[:1, :1, :1, :ROWS, :]))
    lead = lax.dynamic_update_slice(lead, mark, (0, 0, 0, 0, 0))
    rest = exchange(rest)

    beams, visibilities = None, None
    for order, (a, b) in enumerate(cuts):
        if order == len(cuts) - 1:
            if order:
                rest, relays, beams, visibilities = tie((rest, relays, beams, visibilities))
            else:
                rest, relays = tie((rest, relays))
            far = swap(relays[order], half, gx_count)
            beams = beams_of(spot, lead, [rest], weights, turns, 0, 0, main, beams)
        else:
            far = swap(relays[order], half, gx_count)
        parts = near + [far]
        beams = beams_of(spot, lead, parts, weights, turns, main + a, a, b - a, beams)
        if order < len(cuts) - 1:
            visibilities = gram_of(spot, lead, parts, main + a, a, b - a, visibilities)
    if not cuts:
        beams = beams_of(spot, lead, [rest], weights, turns, 0, 0, main, beams)
    spot, beams = tie((spot, beams))
    if beams.ndim == 4:
        beams = beams.reshape(chan_dev, 2, gx_count, -1, beams.shape[3]).transpose(2, 0, 1, 3, 4)
    sums = exchange(beams)
    visibilities = gram_of(spot, lead, [rest], 0, 0, main, visibilities)
    for a, b in cuts[-1:]:
        visibilities = gram_of(spot, lead, parts, main + a, a, b - a, visibilities)
    series = series_of([sums], table_rows)
    return (visibilities, series)


def solution(mesh):
    placed = (P(None, ("groups", "gx"), None), P("gx"), P(), P(), P("groups"), P("groups", None))
    return jax.shard_map(
        shards,
        mesh=mesh,
        in_specs=placed,
        out_specs=(P(("groups", "gx"), None, None), P(None, ("groups", "gx"), None, None)),
        check_vma=False,
    )
```
